32 devices in a mesh: swath: 2 (over x), rng: 16 (over z, y, core).
Axes of the slice: x: 2, y: 2, z: 4, core: 2. Of those that a mesh axis runs over, the one named last changes fastest.
Arguments:
- echoes: float32 [2, 512, 32768], P(None, ('swath', 'rng')), parts along dimension 1, may hold values from -6 to 6
- doppler_filter: float32 [2, 32768], replicated, may hold values from -5 to 5
- migration_shift: int32 [32768], replicated, may hold values from 0 to 9, as said below
- kernel_index: int32 [32768], replicated, may hold values from 0 to 15
- kernel_taps: float32 [16, 16], replicated, may hold values from -1.5 to 1.5
Outputs:
- image: float32 [2, 512, 32768], P(None, ('swath', 'rng')), parts along dimension 1
The draws below stay inside these ranges and needn't reach their ends.
There are 2 independent parts, one for each index of `swath`. The reference program is written for one: setup_inputs(seed, part) draws one part's arguments, and reference() takes and returns one part's arrays. A program takes and returns all parts, laid end to end along the dimension named above; an argument that names none is the same for every part. Nothing has to cross between parts.
Inputs may be any that keep to these rules, and one draw needn't show every extreme that they name: `migration_shift`: both 0 and 9 occur.
All inputs are finite; a program needn't handle non-finite values.
Results may differ from the reference program's by a relative error of at most 0.0041.
Values may be sent and summed in bfloat16 or wider, within the bound.
No kernel may reach another device: no remote copies, remote signals or barrier semaphores. Data moves between devices by JAX's collectives and lax.ppermute only.
A program may use at most 64 MiB of HBM per device.

```python
import math
import jax
import jax.numpy as jnp
from jax import lax

PULSES = 32768
RANGE = 256
TAPS = 16
NKER = 16
SMAX = 9


def draw_migration_shift(key, part):
    key_values, key_top, key_gap = jax.random.split(key, 3)
    values = jax.random.randint(key_values, (PULSES,), 0, SMAX + 1)
    where_top = jax.random.randint(key_top, (), 0, PULSES)
    distance = jax.random.randint(key_gap, (), 1, PULSES)
    where_zero = (where_top + distance) % PULSES
    positions = jnp.arange(PULSES, dtype=jnp.int32)
    values = jnp.where(positions == where_top, SMAX, values)
    return jnp.where(positions == where_zero, 0, values).astype(jnp.int32)


def place_ends(values, rng, low, top_value):
    shape = values.shape
    index_at = [jax.random.randint(jax.random.fold_in(rng, axis), (), 0, shape[axis]) for axis in range(len(shape))]
    values = values.at[tuple(index_at)].set(low)
    longest = shape.index(max(shape))
    index_at[longest] = (index_at[longest] + 1) % shape[longest]
    return values.at[tuple(index_at)].set(top_value)


def block_scale(stream_key, dims, shards, low, top_value):
    def one(axis_at, shards_of):
        draws = jax.random.uniform(jax.random.fold_in(jax.random.fold_in(stream_key, 6), axis_at), (shards_of,), jnp.float32, low / len(shards), top_value / len(shards))
        return jnp.repeat(jnp.exp(draws), dims[axis_at] // shards_of).reshape((-1,) + (1,) * (len(dims) - axis_at - 1))

    level = one(*shards[0])
    for cut in shards[1:]:
        level = level * one(*cut)
    return level


def normal_values(key, dims, deviation, limit, cuts=(), kind=jnp.bfloat16):
    values = jax.random.normal(key, dims, jnp.float32) * deviation
    if len(cuts) > 0:
        values = block_scale(key, dims, cuts, -0.22, 0.18) * values
    return jnp.clip(values, min=-limit, max=limit).astype(kind)


def setup_inputs(seed: int = 0, part: int = 0) -> dict:
    seeds = jax.random.split(jax.random.key(seed), 6)
    own_keys = jax.random.split(jax.random.fold_in(seeds[5], part), 6)
    echoes = normal_values(own_keys[0], (2, RANGE, PULSES), 1.0, 6.0, ((1, 16),), jnp.float32)
    doppler_filter = normal_values(seeds[1], (2, PULSES), 0.7, 5.0, (), jnp.float32)
    migration_shift = draw_migration_shift(jax.random.fold_in(seeds[5], 71), part)
    kernel_index = place_ends(jax.random.randint(seeds[3], (PULSES,), 0, NKER), jax.random.fold_in(seeds[3], 1), 0, NKER - 1).astype(jnp.int32)
    kernel_taps = normal_values(seeds[4], (NKER, TAPS), TAPS ** -0.5, 1.5, (), jnp.float32)
    return dict(echoes=echoes, doppler_filter=doppler_filter, migration_shift=migration_shift, kernel_index=kernel_index, kernel_taps=kernel_taps)


def reference(echoes, doppler_filter, migration_shift, kernel_index, kernel_taps):
    norm_scale = 1.0 / math.sqrt(PULSES)
    samples = lax.complex(echoes[0], echoes[1])
    spectrum = jnp.fft.fft(samples, axis=1) * norm_scale
    response = lax.complex(doppler_filter[0], -doppler_filter[1])
    weighted = spectrum * response[None, :]
    filtered = jnp.stack([jnp.real(weighted), jnp.imag(weighted)]).astype(jnp.bfloat16)
    coefficients = kernel_taps[kernel_index]
    tap_numbers = jnp.arange(TAPS, dtype=jnp.int32)
    low_margin = SMAX + TAPS // 2 - 1
    padded = jnp.pad(filtered, ((0, 0), (low_margin, TAPS // 2), (0, 0)))
    running = jnp.zeros((2, RANGE, PULSES), jnp.float32)
    for offset_slot in range(TAPS + SMAX):
        chosen = (tap_numbers[None, :] == (offset_slot - migration_shift)[:, None]).astype(jnp.float32)
        column_weight = lax.optimization_barrier(jnp.sum(coefficients * chosen, axis=1))
        first_row = low_margin + TAPS // 2 - offset_slot
        segment = padded[:, first_row:first_row + RANGE, :].astype(jnp.float32)
        running = running + column_weight[None, None, :] * segment
    migrated = running.astype(jnp.bfloat16)
    restored = lax.complex(migrated[0].astype(jnp.float32), migrated[1].astype(jnp.float32))
    image_parts = jnp.fft.ifft(restored, axis=1) / norm_scale
    return jnp.stack([jnp.real(image_parts), jnp.imag(image_parts)]).astype(jnp.float32)
```

```python
import functools
import math

import jax
import jax.numpy as jnp
import numpy as np
from jax import lax
from jax.experimental import pallas as pl
from jax.experimental.pallas import tpu as pltpu
from jax.sharding import PartitionSpec as P

LANES = 128
INNER = 256
SUBLANES = 8
SMAX = 9
VMEM_LIMIT = 56 * 1024 * 1024


def split(values):
    high = values.astype(jnp.bfloat16)
    low = (values - high.astype(jnp.float32)).astype(jnp.bfloat16)
    return high, low


def dft_angles(length):
    numbers = np.arange(length, dtype=np.int64)
    return (numbers[:, None] * numbers[None, :] % length) * (2.0 * math.pi / length)


def np_split(values):
    values = values.astype(np.float32)
    high = values.astype(jnp.bfloat16)
    low = (values - high.astype(np.float32)).astype(jnp.bfloat16)
    return high, low


def tables(pulse_count):
    outer = pulse_count // INNER
    outer_angles = dft_angles(outer)
    inner_angles = dft_angles(INNER)
    oc, osn = np.cos(outer_angles), np.sin(outer_angles)
    ic, isn = np.cos(inner_angles), np.sin(inner_angles)
    forward_outer = np.block([[oc, osn], [-osn, oc]])
    forward_inner = np.block([[ic, -isn], [isn, ic]])
    inverse_inner = np.block([[ic, isn], [-isn, ic]])
    inverse_outer = np.block([[oc, -osn], [osn, oc]])
    twist = (
        np.arange(outer, dtype=np.int64)[:, None] * np.arange(INNER, dtype=np.int64)[None, :]
    ) * (2.0 * math.pi / pulse_count)
    scale = 1.0 / math.sqrt(pulse_count)
    twiddle = np.stack([np.cos(twist), np.sin(twist)]) * scale
    return dict(
        forward_outer=np.stack(np_split(forward_outer)),
        forward_inner=np.stack(np_split(forward_inner)),
        inverse_inner=inverse_inner.astype(jnp.bfloat16),
        inverse_outer=inverse_outer.astype(jnp.bfloat16),
        twiddle=twiddle.astype(np.float32),
    )


def forward_kernel(
    echo_ref, outer_ref, inner_ref, twiddle_ref, response_ref, out_ref,
    tiles, response_rows, rotated_high, rotated_low,
):
    rows = echo_ref.shape[1]
    pulse_count = echo_ref.shape[2]
    outer = pulse_count // INNER
    tile_count = pulse_count // LANES
    per_row = INNER // LANES
    for part in range(2):
        for tile in range(tile_count):
            tiles[part, pl.ds(tile * rows, rows), :] = echo_ref[
                part, :, pl.ds(tile * LANES, LANES)
            ]
    for tile in range(tile_count):
        response_rows[pl.ds(tile * 2, 2), :] = response_ref[:, pl.ds(tile * LANES, LANES)]
    outer_high, outer_low = outer_ref[0], outer_ref[1]
    cosine, sine = twiddle_ref[0], twiddle_ref[1]
    for row in range(rows):
        signal = jnp.concatenate(
            [
                jnp.concatenate(
                    [
                        tiles[part, pl.ds(half * rows + row, outer, stride=per_row * rows), :]
                        for half in range(per_row)
                    ],
                    axis=1,
                )
                for part in range(2)
            ],
            axis=0,
        )
        high, low = split(signal)
        sectioned = (
            jnp.dot(outer_high, low, preferred_element_type=jnp.float32)
            + jnp.dot(outer_low, high, preferred_element_type=jnp.float32)
            + jnp.dot(outer_high, high, preferred_element_type=jnp.float32)
        )
        real, imag = sectioned[:outer], sectioned[outer:]
        place = pl.ds(row * outer, outer)
        high, low = split(real * cosine + imag * sine)
        rotated_high[place, :INNER] = high
        rotated_low[place, :INNER] = low
        high, low = split(imag * cosine - real * sine)
        rotated_high[place, INNER:] = high
        rotated_low[place, INNER:] = low
    response_real = response_rows[pl.ds(0, tile_count, stride=2), :].T
    response_imag = response_rows[pl.ds(1, tile_count, stride=2), :].T
    inner_high, inner_low = inner_ref[0], inner_ref[1]
    step = 2 * outer
    for start in range(0, rows * outer, step):
        high = rotated_high[pl.ds(start, step), :]
        low = rotated_low[pl.ds(start, step), :]
        spectrum = (
            jnp.dot(high, inner_low, preferred_element_type=jnp.float32)
            + jnp.dot(low, inner_high, preferred_element_type=jnp.float32)
            + jnp.dot(high, inner_high, preferred_element_type=jnp.float32)
        )
        for index in range(step // outer):
            row = start // outer + index
            real = spectrum[index * outer : (index + 1) * outer, :INNER]
            imag = spectrum[index * outer : (index + 1) * outer, INNER:]
            out_ref[0, row] = (real * response_real + imag * response_imag).astype(jnp.bfloat16)
            out_ref[1, row] = (imag * response_real - real * response_imag).astype(jnp.bfloat16)


def forward(echoes, doppler_filter, table, block):
    pulse_count = echoes.shape[2]
    rows = SUBLANES
    outer = pulse_count // INNER
    whole = lambda array: pl.BlockSpec(array.shape, lambda i: (0,) * array.ndim)
    operands = [table["forward_outer"], table["forward_inner"], table["twiddle"], doppler_filter]
    return pl.pallas_call(
        forward_kernel,
        grid=(1,),
        out_shape=jax.ShapeDtypeStruct((2, rows, outer, INNER), jnp.bfloat16),
        in_specs=[pl.BlockSpec((2, rows, pulse_count), lambda i: (0, block, 0))]
        + [whole(array) for array in operands],
        out_specs=pl.BlockSpec((2, rows, outer, INNER), lambda i: (0, 0, 0, 0)),
        scratch_shapes=[
            pltpu.VMEM((2, pulse_count // LANES * rows, LANES), jnp.float32),
            pltpu.VMEM((pulse_count // LANES * 2, LANES), jnp.float32),
            pltpu.VMEM((rows * outer, 2 * INNER), jnp.bfloat16),
            pltpu.VMEM((rows * outer, 2 * INNER), jnp.bfloat16),
        ],
        compiler_params=pltpu.CompilerParams(vmem_limit_bytes=VMEM_LIMIT),
        cost_estimate=pl.CostEstimate(
            flops=6 * rows * pulse_count * (2 * outer + 2 * INNER),
            bytes_accessed=12 * rows * pulse_count,
            transcendentals=0,
        ),
        name="forward_dft",
    )(echoes, *operands)


def image_kernel(
    *refs, block_count, aliased,
):
    blocks = refs[:block_count]
    shift_ref, kernel_ref, taps_ref, inner_ref, outer_ref, twiddle_ref = refs[
        block_count : block_count + 6
    ]
    out_ref, migrated, shifts, kernels, tiles = refs[block_count + 6 + aliased :]
    rows = out_ref.shape[1]
    pulse_count = out_ref.shape[2]
    outer = pulse_count // INNER
    tile_count = pulse_count // LANES
    per_row = INNER // LANES
    tap_count = taps_ref.shape[0]
    half_taps = tap_count // 2
    shifts[...] = shift_ref[...].T
    kernels[...] = kernel_ref[...].T
    reach = SMAX + half_taps - 1
    input_rows = block_count * rows
    first = reach + half_taps - tap_count + 1
    group = 2 * SUBLANES

    def migrate(step, carry):
        sub = pl.multiple_of(step * group, group)
        for half in range(per_row):
            lanes = pl.ds(half * LANES, LANES)
            shift = shifts[pl.ds(sub, group), lanes]
            kernel_index = kernels[pl.ds(sub, group), lanes]
            bits = [
                ((shift // (1 << bit)) % 2).astype(jnp.float32).astype(jnp.bfloat16)
                > jnp.bfloat16(0.5)
                for bit in range(SMAX.bit_length())
            ]
            coefficients = [
                jnp.take_along_axis(
                    jnp.broadcast_to(taps_ref[pl.ds(tap, 1), :], (group, LANES)),
                    kernel_index,
                    axis=1,
                )
                for tap in range(tap_count)
            ]
            for part in range(2):
                moved = [
                    blocks[row // rows][part, row % rows, pl.ds(sub, group), lanes]
                    for row in range(input_rows)
                ]
                for bit in reversed(range(len(bits))):
                    jump = 1 << bit
                    low = first - (jump - 1)
                    moved = [
                        jnp.where(bits[bit], moved[row - jump], moved[row])
                        if row >= max(low, jump)
                        else moved[row]
                        for row in range(input_rows)
                    ]
                wide = {row: moved[row].astype(jnp.float32) for row in range(first, input_rows)}
                for row in range(rows):
                    total = None
                    for tap in range(tap_count):
                        term = coefficients[tap] * wide[row + reach + half_taps - tap]
                        total = term if total is None else total + term
                    migrated[
                        pl.ds(pl.multiple_of(row * outer + sub, group), group),
                        pl.ds(part * INNER + half * LANES, LANES),
                    ] = total.astype(jnp.bfloat16)
        return carry

    lax.fori_loop(0, outer // group, migrate, 0)
    cosine, sine = twiddle_ref[0], twiddle_ref[1]
    step = 2 * outer
    for start in range(0, rows * outer, step):
        sectioned = jnp.dot(
            migrated[pl.ds(start, step), :], inner_ref[...], preferred_element_type=jnp.float32
        )
        for index in range(step // outer):
            row = start // outer + index
            real = sectioned[index * outer : (index + 1) * outer, :INNER]
            imag = sectioned[index * outer : (index + 1) * outer, INNER:]
            turned = jnp.concatenate(
                [
                    (real * cosine - imag * sine).astype(jnp.bfloat16),
                    (real * sine + imag * cosine).astype(jnp.bfloat16),
                ],
                axis=0,
            )
            image = jnp.dot(outer_ref[...], turned, preferred_element_type=jnp.float32)
            for part in range(2):
                for half in range(per_row):
                    tiles[part, pl.ds(half * rows + row, outer, stride=per_row * rows), :] = image[
                        part * outer : (part + 1) * outer, half * LANES : (half + 1) * LANES
                    ]
    for part in range(2):
        for tile in range(tile_count):
            out_ref[part, :, pl.ds(tile * LANES, LANES)] = tiles[
                part, pl.ds(tile * rows, rows), :
            ]


def image(blocks, shift, kernel_index, taps, table, block, shape, previous):
    row_count, pulse_count = shape
    rows = SUBLANES
    outer = pulse_count // INNER
    whole = lambda array: pl.BlockSpec(array.shape, lambda i: (0,) * array.ndim)
    operands = [
        *blocks, shift, kernel_index, taps,
        table["inverse_inner"], table["inverse_outer"], table["twiddle"],
    ]
    specs = [whole(array) for array in operands]
    aliases = {}
    if previous is not None:
        aliases = {len(operands): 0}
        operands.append(previous)
        specs.append(pl.BlockSpec(memory_space=pl.ANY))
    return pl.pallas_call(
        functools.partial(
            image_kernel, block_count=len(blocks), aliased=int(previous is not None)
        ),
        grid=(1,),
        out_shape=jax.ShapeDtypeStruct((2, row_count, pulse_count), jnp.float32),
        in_specs=specs,
        out_specs=pl.BlockSpec((2, rows, pulse_count), lambda i: (0, block, 0)),
        input_output_aliases=aliases,
        scratch_shapes=[
            pltpu.VMEM((rows * outer, 2 * INNER), jnp.bfloat16),
            pltpu.VMEM((outer, INNER), jnp.int32),
            pltpu.VMEM((outer, INNER), jnp.int32),
            pltpu.VMEM((2, pulse_count // LANES * rows, LANES), jnp.float32),
        ],
        compiler_params=pltpu.CompilerParams(vmem_limit_bytes=VMEM_LIMIT),
        cost_estimate=pl.CostEstimate(
            flops=8 * rows * pulse_count * (2 * outer + 2 * INNER),
            bytes_accessed=24 * rows * pulse_count,
            transcendentals=0,
        ),
        name="migrate_and_image",
    )(*operands)


def per_device(echoes, doppler_filter, migration_shift, kernel_index, kernel_taps):
    row_count = echoes.shape[1]
    pulse_count = echoes.shape[2]
    outer = pulse_count // INNER
    rows = SUBLANES
    table = tables(pulse_count)
    count = lax.axis_size("rng")
    ahead = [(i, i + 1) for i in range(count - 1)]
    back = [(i + 1, i) for i in range(count - 1)]

    upper = forward(echoes, doppler_filter, table, 1)
    left_upper = lax.ppermute(upper, "rng", ahead)
    lower = forward(echoes, doppler_filter, table, 0)
    right_lower = lax.ppermute(lower, "rng", back)
    left_lower = lax.ppermute(lower, "rng", ahead)

    shift = migration_shift.reshape(INNER, outer)
    index = kernel_index.reshape(INNER, outer)
    taps = jnp.pad(kernel_taps.T, ((0, 0), (0, LANES - kernel_taps.shape[0])))
    shape = (row_count, pulse_count)
    picture = image(
        [left_upper, lower, upper, right_lower], shift, index, taps, table, 1, shape, None
    )
    return image(
        [left_lower, left_upper, lower, upper], shift, index, taps, table, 0, shape, picture
    )


def solution(mesh):
    return jax.shard_map(
        per_device,
        mesh=mesh,
        in_specs=(P(None, ("swath", "rng"), None), P(), P(), P(), P()),
        out_specs=P(None, ("swath", "rng"), None),
        check_vma=False,
    )
```

```python
import functools
import math

import jax
import jax.numpy as jnp
import numpy as np
from jax import lax
from jax.experimental import pallas as pl
from jax.experimental.pallas import tpu as pltpu
from jax.sharding import PartitionSpec as P

LANES = 128
INNER = 256
SUBLANES = 8
SMAX = 9
PER = 2
VMEM_LIMIT = 24 * 1024 * 1024
VMEM_ALL = 56 * 1024 * 1024


def split(values):
    high = values.astype(jnp.bfloat16)
    low = (values - high.astype(jnp.float32)).astype(jnp.bfloat16)
    return high, low


def dft_angles(length):
    numbers = np.arange(length, dtype=np.int64)
    return (numbers[:, None] * numbers[None, :] % length) * (2.0 * math.pi / length)


def np_split(values):
    values = values.astype(np.float32)
    high = values.astype(jnp.bfloat16)
    low = (values - high.astype(np.float32)).astype(jnp.bfloat16)
    return high, low


def tables(pulse_count):
    outer = pulse_count // INNER
    half = INNER // 2
    outer_angles = dft_angles(outer)
    oc, osn = np.cos(outer_angles), np.sin(outer_angles)
    places = np.arange(half, dtype=np.int64)
    forward_inner, inverse_inner = [], []
    for parity in range(2):
        angles = (places[:, None] * (2 * places[None, :] + parity) % INNER) * (
            2.0 * math.pi / INNER
        )
        ic, isn = np.cos(angles), np.sin(angles)
        forward_inner.append(np.stack(np_split(np.block([[ic, -isn], [isn, ic]]))))
        inverse_inner.append(np.block([[ic.T, isn.T], [-isn.T, ic.T]]).astype(jnp.bfloat16))
    forward_outer = np.block([[oc, osn], [-osn, oc]])
    inverse_outer = np.block([[oc, -osn], [osn, oc]])
    twist = (
        np.arange(outer, dtype=np.int64)[:, None] * np.arange(INNER, dtype=np.int64)[None, :]
    ) * (2.0 * math.pi / pulse_count)
    scale = 1.0 / math.sqrt(pulse_count)
    twiddle = np.stack([np.cos(twist), np.sin(twist)]) * scale
    return dict(
        forward_outer=np.stack(np_split(forward_outer)),
        forward_inner=np.stack(forward_inner),
        inverse_inner=np.stack(inverse_inner),
        inverse_outer=inverse_outer.astype(jnp.bfloat16),
        twiddle=twiddle.astype(np.float32),
    )


def forward_kernel(
    echo_hbm, outer_hbm, inner_hbm, twiddle_hbm, response_hbm, out_hbm,
    echo, outer_table, inner_table, twiddle, response, response_rows,
    signal_high, signal_low, rotated_high, rotated_low, out, semaphores, *, block
):
    rows = out.shape[1]
    pulse_count = echo.shape[2]
    outer = pulse_count // INNER
    half = INNER // 2
    chunks = 8
    chunk = pulse_count // chunks
    ready = [
        pltpu.make_async_copy(source, target, semaphores.at[index])
        for index, (source, target) in enumerate(
            [
                (response_hbm, response),
                (outer_hbm, outer_table),
                (twiddle_hbm, twiddle),
                (inner_hbm, inner_table),
            ]
        )
    ]
    for index in range(chunks):
        place = pl.ds(index * chunk, chunk)
        ready.append(
            pltpu.make_async_copy(
                echo_hbm.at[:, pl.ds(block * rows, rows), place],
                echo.at[:, :, place],
                semaphores.at[4 + index],
            )
        )
    for index in [0, *range(4, 4 + chunks), 1, 2, 3]:
        ready[index].start()
    ready[0].wait()
    for tile in range(INNER):
        response_rows[pl.ds(tile * 2, 2), :] = response[:, pl.ds(tile * outer, outer)]
    response_parts = [
        [response_rows[pl.ds(2 * parity + part, half, stride=4), :].T for part in range(2)]
        for parity in range(2)
    ]
    for index in range(chunks):
        ready[4 + index].wait()
        for part in range(2):
            for first in range(index * outer // chunks, (index + 1) * outer // chunks, SUBLANES):
                gathered = jnp.stack(
                    [
                        echo[part, :, pl.ds((first + offset) * INNER, INNER)]
                        for offset in range(SUBLANES)
                    ]
                )
                high, low = split(jnp.swapaxes(gathered, 0, 1))
                place = pl.ds(part * outer + first, SUBLANES)
                signal_high[:, place, :] = high
                signal_low[:, place, :] = low
    ready[1].wait()
    ready[2].wait()
    outer_high, outer_low = outer_table[0], outer_table[1]
    cosine, sine = twiddle[0], twiddle[1]

    def first_stage(row):
        high, low = signal_high[row], signal_low[row]
        sectioned = (
            jnp.dot(outer_high, low, preferred_element_type=jnp.float32)
            + jnp.dot(outer_low, high, preferred_element_type=jnp.float32)
            + jnp.dot(outer_high, high, preferred_element_type=jnp.float32)
        )
        real, imag = sectioned[:outer], sectioned[outer:]
        turned = (real * cosine + imag * sine, imag * cosine - real * sine)
        place = pl.ds(row * outer, outer)
        for part in range(2):
            left, right = turned[part][:, :half], turned[part][:, half:]
            for parity, value in enumerate((left + right, left - right)):
                high, low = split(value)
                lanes = pl.ds((2 * parity + part) * half, half)
                rotated_high[place, lanes] = high
                rotated_low[place, lanes] = low

    def second_stage(row):
        place = pl.ds(row * outer, PER * outer)
        for parity in range(2):
            lanes = pl.ds(parity * INNER, INNER)
            high = rotated_high[place, lanes]
            low = rotated_low[place, lanes]
            table_high, table_low = inner_table[parity, 0], inner_table[parity, 1]
            spectrum = (
                jnp.dot(high, table_low, preferred_element_type=jnp.float32)
                + jnp.dot(low, table_high, preferred_element_type=jnp.float32)
                + jnp.dot(high, table_high, preferred_element_type=jnp.float32)
            )
            response_real, response_imag = response_parts[parity]
            lanes = pl.ds(parity * half, half)
            for index in range(PER):
                real = spectrum[index * outer : (index + 1) * outer, :half]
                imag = spectrum[index * outer : (index + 1) * outer, half:]
                out[0, row + index, :, lanes] = (
                    real * response_real + imag * response_imag
                ).astype(jnp.bfloat16)
                out[1, row + index, :, lanes] = (
                    imag * response_real - real * response_imag
                ).astype(jnp.bfloat16)
        place = pl.ds(row, PER)
        leaving = pltpu.make_async_copy(
            out.at[:, place], out_hbm.at[:, place], semaphores.at[4 + row // PER]
        )
        leaving.start()
        return leaving

    leaving = []
    for row in range(rows):
        first_stage(row)
        if row == 1:
            ready[3].wait()
        if row % PER == PER - 1 and row >= PER:
            leaving.append(second_stage(row + 1 - 2 * PER))
    leaving.append(second_stage(rows - PER))
    for copy in leaving:
        copy.wait()


def forward(echoes, doppler_filter, table, block):
    pulse_count = echoes.shape[2]
    rows = SUBLANES
    outer = pulse_count // INNER
    operands = [table["forward_outer"], table["forward_inner"], table["twiddle"], doppler_filter]
    anywhere = pl.BlockSpec(memory_space=pl.ANY)
    return pl.pallas_call(
        functools.partial(forward_kernel, block=block),
        out_shape=jax.ShapeDtypeStruct((2, rows, outer, INNER), jnp.bfloat16),
        in_specs=[anywhere] * 5,
        out_specs=anywhere,
        scratch_shapes=[
            pltpu.VMEM((2, rows, pulse_count), jnp.float32),
            *[pltpu.VMEM(array.shape, array.dtype) for array in operands],
            pltpu.VMEM((2 * INNER, outer), jnp.float32),
            pltpu.VMEM((rows, 2 * outer, INNER), jnp.bfloat16),
            pltpu.VMEM((rows, 2 * outer, INNER), jnp.bfloat16),
            pltpu.VMEM((rows * outer, 2 * INNER), jnp.bfloat16),
            pltpu.VMEM((rows * outer, 2 * INNER), jnp.bfloat16),
            pltpu.VMEM((2, rows, outer, INNER), jnp.bfloat16),
            pltpu.SemaphoreType.DMA((12,)),
        ],
        compiler_params=pltpu.CompilerParams(vmem_limit_bytes=VMEM_ALL),
        cost_estimate=pl.CostEstimate(
            flops=6 * rows * pulse_count * (2 * outer + INNER),
            bytes_accessed=12 * rows * pulse_count,
            transcendentals=0,
        ),
        name="forward_dft",
    )(echoes, *operands)


def migrate(inputs, known, taps, shifts, kernels, rows, store):
    outer = shifts.shape[0]
    half = INNER // 2
    tap_count = taps.shape[0]
    half_taps = tap_count // 2
    group = 2 * SUBLANES
    reach = SMAX + half_taps - 1
    input_rows = len(known) * rows
    first = reach + half_taps - tap_count + 1
    present = [known[row // rows] for row in range(input_rows)]

    def body(step, carry):
        sub = pl.multiple_of(step * group, group)
        for parity in range(2):
            lanes = pl.ds(parity * half, half)
            shift_here = shifts[pl.ds(sub, group), lanes]
            kernel_here = kernels[pl.ds(sub, group), lanes]
            bits = [
                ((shift_here // (1 << bit)) % 2).astype(jnp.float32).astype(jnp.bfloat16)
                > jnp.bfloat16(0.5)
                for bit in range(SMAX.bit_length())
            ]
            coefficients = [
                jnp.take_along_axis(
                    jnp.broadcast_to(taps[pl.ds(tap, 1), :], (group, LANES)), kernel_here, axis=1
                )
                for tap in range(tap_count)
            ]
            nothing = jnp.zeros((group, LANES), jnp.bfloat16)
            for part in range(2):
                moved = [
                    inputs[row // rows][part, row % rows, pl.ds(sub, group), lanes]
                    if present[row]
                    else None
                    for row in range(input_rows)
                ]
                for bit in reversed(range(len(bits))):
                    jump = 1 << bit
                    low = first - (jump - 1)
                    later = []
                    for row in range(input_rows):
                        here = moved[row]
                        if row >= max(low, jump):
                            there = moved[row - jump]
                            if here is not None or there is not None:
                                here = jnp.where(
                                    bits[bit],
                                    nothing if there is None else there,
                                    nothing if here is None else here,
                                )
                        later.append(here)
                    moved = later
                wide = {
                    row: moved[row].astype(jnp.float32)
                    for row in range(first, input_rows)
                    if any(present[max(row - SMAX, 0) : row + 1])
                }
                for row in range(rows):
                    total = None
                    for tap in range(tap_count):
                        source = row + reach + half_taps - tap
                        if source in wide:
                            term = coefficients[tap] * wide[source]
                            total = term if total is None else total + term
                    store(part, parity, row, pl.ds(sub, group), total)
        return carry

    lax.fori_loop(0, outer // group, body, 0)


def order_indices(shift, kernel, shifts, kernels):
    half = INNER // 2
    for parity in range(2):
        lanes = pl.ds(parity * half, half)
        shifts[:, lanes] = shift[pl.ds(parity, half, stride=2), :].T
        kernels[:, lanes] = kernel[pl.ds(parity, half, stride=2), :].T


def partial_kernel(*refs, known, has_partial):
    count = sum(known)
    earlier = refs[count] if has_partial else None
    shift, kernel, taps, out, shifts, kernels = refs[count + has_partial :]
    half = INNER // 2
    blocks = iter(refs[:count])
    inputs = [next(blocks) if there else None for there in known]
    order_indices(shift, kernel, shifts, kernels)

    def store(part, parity, row, place, total):
        lanes = pl.ds(parity * half, half)
        if has_partial:
            before = earlier[part, row, place, lanes]
            total = before if total is None else total + before
        out[part, row, place, lanes] = total

    migrate(inputs, known, taps, shifts, kernels, out.shape[1], store)


def partial(blocks, known, shift, kernel_index, taps, earlier):
    operands = [*blocks, *([] if earlier is None else [earlier]), shift, kernel_index, taps]
    rows, outer = blocks[0].shape[1], blocks[0].shape[2]
    inside = pl.BlockSpec(memory_space=pltpu.VMEM)
    return pl.pallas_call(
        functools.partial(
            partial_kernel, known=known, has_partial=int(earlier is not None)
        ),
        out_shape=jax.ShapeDtypeStruct(blocks[0].shape, jnp.float32),
        in_specs=[inside] * len(operands),
        out_specs=inside,
        scratch_shapes=[
            pltpu.VMEM((outer, INNER), jnp.int32),
            pltpu.VMEM((outer, INNER), jnp.int32),
        ],
        compiler_params=pltpu.CompilerParams(vmem_limit_bytes=VMEM_LIMIT),
        cost_estimate=pl.CostEstimate(
            flops=8 * rows * outer * INNER * 500,
            bytes_accessed=24 * rows * outer * INNER,
            transcendentals=0,
        ),
        name="migrate_known_rows",
    )(*operands)


def image_kernel(*refs, known, has_partial, aliased, block):
    count = sum(known)
    blocks = iter(refs[:count])
    inputs = [next(blocks) if there else None for there in known]
    earlier = refs[count] if has_partial else None
    count += has_partial
    shift, kernel, taps, inner_table, outer_table, twiddle = refs[count : count + 6]
    out_hbm, shifts, kernels, migrated, images, out, semaphores = refs[count + 6 + aliased :]
    rows = out.shape[1]
    pulse_count = out.shape[2]
    outer = pulse_count // INNER
    half = INNER // 2
    order_indices(shift, kernel, shifts, kernels)

    def store(part, parity, row, place, total):
        if has_partial:
            before = earlier[part, row, place, pl.ds(parity * half, half)]
            total = before if total is None else total + before
        migrated[row, place, pl.ds((2 * parity + part) * half, half)] = total.astype(jnp.bfloat16)

    migrate(inputs, known, taps, shifts, kernels, rows, store)
    cosine, sine = twiddle[0], twiddle[1]
    for start in range(0, rows, PER):
        left_parts, right_parts = (
            migrated[pl.ds(start, PER), :, pl.ds(parity * INNER, INNER)].reshape(PER * outer, INNER)
            for parity in range(2)
        )
        even = jnp.dot(left_parts, inner_table[0], preferred_element_type=jnp.float32)
        odd = jnp.dot(right_parts, inner_table[1], preferred_element_type=jnp.float32)
        left, right = even + odd, even - odd
        for index in range(PER):
            here = slice(index * outer, (index + 1) * outer)
            turned = [], []
            for side, value in enumerate((left, right)):
                lanes = slice(side * half, (side + 1) * half)
                real, imag = value[here, :half], value[here, half:]
                turned[0].append(real * cosine[:, lanes] - imag * sine[:, lanes])
                turned[1].append(real * sine[:, lanes] + imag * cosine[:, lanes])
            turned = jnp.concatenate(
                [jnp.concatenate(pair, axis=1).astype(jnp.bfloat16) for pair in turned], axis=0
            )
            images[start + index] = jnp.dot(
                outer_table[...], turned, preferred_element_type=jnp.float32
            )
    chunks = 4
    chunk = pulse_count // chunks
    leaving = []
    for index in range(chunks):
        for part in range(2):
            for first_place in range(
                index * outer // chunks, (index + 1) * outer // chunks, SUBLANES
            ):
                swapped = jnp.swapaxes(
                    images[:, pl.ds(part * outer + first_place, SUBLANES), :], 0, 1
                )
                for offset in range(SUBLANES):
                    out[part, :, pl.ds((first_place + offset) * INNER, INNER)] = swapped[offset]
        place = pl.ds(index * chunk, chunk)
        leaving.append(
            pltpu.make_async_copy(
                out.at[:, :, place],
                out_hbm.at[:, pl.ds(block * rows, rows), place],
                semaphores.at[index],
            )
        )
        leaving[-1].start()
    for copy in leaving:
        copy.wait()


def image(blocks, known, shift, kernel_index, taps, table, block, shape, earlier, previous):
    row_count, pulse_count = shape
    rows = SUBLANES
    outer = pulse_count // INNER
    operands = [
        *blocks, *([] if earlier is None else [earlier]), shift, kernel_index, taps,
        table["inverse_inner"], table["inverse_outer"], table["twiddle"],
    ]
    specs = [pl.BlockSpec(memory_space=pltpu.VMEM)] * len(operands)
    aliases = {}
    anywhere = pl.BlockSpec(memory_space=pl.ANY)
    if previous is not None:
        aliases = {len(operands): 0}
        operands.append(previous)
        specs.append(anywhere)
    return pl.pallas_call(
        functools.partial(
            image_kernel, known=known, has_partial=int(earlier is not None),
            aliased=len(aliases), block=block,
        ),
        out_shape=jax.ShapeDtypeStruct((2, row_count, pulse_count), jnp.float32),
        in_specs=specs,
        out_specs=anywhere,
        input_output_aliases=aliases,
        scratch_shapes=[
            pltpu.VMEM((outer, INNER), jnp.int32),
            pltpu.VMEM((outer, INNER), jnp.int32),
            pltpu.VMEM((rows, outer, 2 * INNER), jnp.bfloat16),
            pltpu.VMEM((rows, 2 * outer, INNER), jnp.float32),
            pltpu.VMEM((2, rows, pulse_count), jnp.float32),
            pltpu.SemaphoreType.DMA((4,)),
        ],
        compiler_params=pltpu.CompilerParams(vmem_limit_bytes=VMEM_LIMIT),
        cost_estimate=pl.CostEstimate(
            flops=8 * rows * pulse_count * (2 * outer + 2 * INNER),
            bytes_accessed=24 * rows * pulse_count,
            transcendentals=0,
        ),
        name="migrate_and_image",
    )(*operands)


def per_device(echoes, doppler_filter, migration_shift, kernel_index, kernel_taps):
    row_count = echoes.shape[1]
    pulse_count = echoes.shape[2]
    outer = pulse_count // INNER
    table = tables(pulse_count)
    count = lax.axis_size("rng")
    ahead = [(i, i + 1) for i in range(count - 1)]
    back = [(i + 1, i) for i in range(count - 1)]
    shift = migration_shift.reshape(INNER, outer)
    index = kernel_index.reshape(INNER, outer)
    taps = jnp.pad(kernel_taps.T, ((0, 0), (0, LANES - kernel_taps.shape[0])))
    shape = (row_count, pulse_count)

    upper = forward(echoes, doppler_filter, table, 1)
    left_upper = lax.ppermute(upper, "rng", ahead)
    lower = forward(echoes, doppler_filter, table, 0)
    right_lower = lax.ppermute(lower, "rng", back)
    high_part = partial([lower, upper], (False, True, True, False), shift, index, taps, None)
    low_part = partial([lower, upper], (False, False, True, True), shift, index, taps, None)
    lower_again, high_part, low_part = lax.optimization_barrier((lower, high_part, low_part))
    left_lower = lax.ppermute(lower_again, "rng", ahead)
    picture = image(
        [left_upper, right_lower], (True, False, False, True),
        shift, index, taps, table, 1, shape, high_part, None,
    )
    low_part = partial(
        [left_upper], (False, True, False, False), shift, index, taps, low_part
    )
    return image(
        [left_lower], (True, False, False, False),
        shift, index, taps, table, 0, shape, low_part, picture,
    )


def solution(mesh):
    return jax.shard_map(
        per_device,
        mesh=mesh,
        in_specs=(P(None, ("swath", "rng"), None), P(), P(), P(), P()),
        out_specs=P(None, ("swath", "rng"), None),
        check_vma=False,
    )
```

```python
import functools
import math

import jax
import jax.numpy as jnp
import numpy as np
from jax import lax
from jax.experimental import pallas as pl
from jax.experimental.pallas import tpu as pltpu
from jax.sharding import PartitionSpec as P

LANES = 128
INNER = 256
SUBLANES = 8
SMAX = 9
PER = 2
ROW_GROUP = 8
VMEM_LIMIT = 24 * 1024 * 1024
VMEM_ALL = 56 * 1024 * 1024


def split(values):
    high = values.astype(jnp.bfloat16)
    low = (values - high.astype(jnp.float32)).astype(jnp.bfloat16)
    return high, low


def dft_angles(length):
    numbers = np.arange(length, dtype=np.int64)
    return (numbers[:, None] * numbers[None, :] % length) * (2.0 * math.pi / length)


def np_split(values):
    values = values.astype(np.float32)
    high = values.astype(jnp.bfloat16)
    low = (values - high.astype(np.float32)).astype(jnp.bfloat16)
    return high, low


def tables(pulse_count):
    outer = pulse_count // INNER
    half = INNER // 2
    outer_angles = dft_angles(outer)
    oc, osn = np.cos(outer_angles), np.sin(outer_angles)
    places = np.arange(half, dtype=np.int64)
    forward_inner, inverse_inner = [], []
    for parity in range(2):
        angles = (places[:, None] * (2 * places[None, :] + parity) % INNER) * (
            2.0 * math.pi / INNER
        )
        ic, isn = np.cos(angles), np.sin(angles)
        forward_inner.append(np.stack(np_split(np.block([[ic, -isn], [isn, ic]]))))
        inverse_inner.append(np.block([[ic.T, isn.T], [-isn.T, ic.T]]).astype(jnp.bfloat16))
    forward_outer = np.block([[oc, osn], [-osn, oc]])
    inverse_outer = np.block([[oc, -osn], [osn, oc]])
    twist = (
        np.arange(outer, dtype=np.int64)[:, None] * np.arange(INNER, dtype=np.int64)[None, :]
    ) * (2.0 * math.pi / pulse_count)
    scale = 1.0 / math.sqrt(pulse_count)
    twiddle = np.stack([np.cos(twist), np.sin(twist)]) * scale
    return dict(
        forward_outer=np.stack(np_split(forward_outer)),
        forward_inner=np.stack(forward_inner),
        inverse_inner=np.stack(inverse_inner),
        inverse_outer=inverse_outer.astype(jnp.bfloat16),
        twiddle=twiddle.astype(np.float32),
    )


def forward_kernel(
    echo_hbm, outer_hbm, inner_hbm, twiddle_hbm, response_hbm, out_hbm,
    echo, outer_table, inner_table, twiddle, response, response_rows,
    signal_high, signal_low, rotated_high, rotated_low, out, semaphores, *, block
):
    rows = out.shape[1]
    pulse_count = echo.shape[2]
    outer = pulse_count // INNER
    half = INNER // 2
    chunks = 8
    chunk = pulse_count // chunks
    ready = [
        pltpu.make_async_copy(source, target, semaphores.at[index])
        for index, (source, target) in enumerate(
            [
                (response_hbm, response),
                (outer_hbm, outer_table),
                (twiddle_hbm, twiddle),
                (inner_hbm, inner_table),
            ]
        )
    ]
    for index in range(chunks):
        place = pl.ds(index * chunk, chunk)
        ready.append(
            pltpu.make_async_copy(
                echo_hbm.at[:, pl.ds(block * rows, rows), place],
                echo.at[:, :, place],
                semaphores.at[4 + index],
            )
        )
    for index in [0, *range(4, 4 + chunks), 1, 2, 3]:
        ready[index].start()
    ready[0].wait()
    for tile in range(INNER):
        response_rows[pl.ds(tile * 2, 2), :] = response[:, pl.ds(tile * outer, outer)]
    response_parts = [
        [response_rows[pl.ds(2 * parity + part, half, stride=4), :].T for part in range(2)]
        for parity in range(2)
    ]
    for index in range(chunks):
        ready[4 + index].wait()
        for part in range(2):
            for first in range(index * outer // chunks, (index + 1) * outer // chunks, SUBLANES):
                gathered = jnp.stack(
                    [
                        echo[part, :, pl.ds((first + offset) * INNER, INNER)]
                        for offset in range(SUBLANES)
                    ]
                )
                high, low = split(jnp.swapaxes(gathered, 0, 1))
                place = pl.ds(part * outer + first, SUBLANES)
                signal_high[:, place, :] = high
                signal_low[:, place, :] = low
    ready[1].wait()
    ready[2].wait()
    outer_high, outer_low = outer_table[0], outer_table[1]
    cosine, sine = twiddle[0], twiddle[1]

    def first_stage(row):
        high, low = signal_high[row], signal_low[row]
        sectioned = (
            jnp.dot(outer_high, low, preferred_element_type=jnp.float32)
            + jnp.dot(outer_low, high, preferred_element_type=jnp.float32)
            + jnp.dot(outer_high, high, preferred_element_type=jnp.float32)
        )
        real, imag = sectioned[:outer], sectioned[outer:]
        turned = (real * cosine + imag * sine, imag * cosine - real * sine)
        place = pl.ds(row * outer, outer)
        for part in range(2):
            left, right = turned[part][:, :half], turned[part][:, half:]
            for parity, value in enumerate((left + right, left - right)):
                high, low = split(value)
                lanes = pl.ds((2 * parity + part) * half, half)
                rotated_high[place, lanes] = high
                rotated_low[place, lanes] = low

    def second_stage(row):
        place = pl.ds(row * outer, PER * outer)
        for parity in range(2):
            lanes = pl.ds(parity * INNER, INNER)
            high = rotated_high[place, lanes]
            low = rotated_low[place, lanes]
            table_high, table_low = inner_table[parity, 0], inner_table[parity, 1]
            spectrum = (
                jnp.dot(high, table_low, preferred_element_type=jnp.float32)
                + jnp.dot(low, table_high, preferred_element_type=jnp.float32)
                + jnp.dot(high, table_high, preferred_element_type=jnp.float32)
            )
            response_real, response_imag = response_parts[parity]
            lanes = pl.ds(parity * half, half)
            for index in range(PER):
                real = spectrum[index * outer : (index + 1) * outer, :half]
                imag = spectrum[index * outer : (index + 1) * outer, half:]
                out[0, row + index, :, lanes] = (
                    real * response_real + imag * response_imag
                ).astype(jnp.bfloat16)
                out[1, row + index, :, lanes] = (
                    imag * response_real - real * response_imag
                ).astype(jnp.bfloat16)
        place = pl.ds(row, PER)
        leaving = pltpu.make_async_copy(
            out.at[:, place], out_hbm.at[:, place], semaphores.at[4 + row // PER]
        )
        leaving.start()
        return leaving

    leaving = []
    for row in range(rows):
        first_stage(row)
        if row == 1:
            ready[3].wait()
        if row % PER == PER - 1 and row >= PER:
            leaving.append(second_stage(row + 1 - 2 * PER))
    leaving.append(second_stage(rows - PER))
    for copy in leaving:
        copy.wait()


def forward(echoes, doppler_filter, table, block):
    pulse_count = echoes.shape[2]
    rows = SUBLANES
    outer = pulse_count // INNER
    operands = [table["forward_outer"], table["forward_inner"], table["twiddle"], doppler_filter]
    anywhere = pl.BlockSpec(memory_space=pl.ANY)
    return pl.pallas_call(
        functools.partial(forward_kernel, block=block),
        out_shape=jax.ShapeDtypeStruct((2, rows, outer, INNER), jnp.bfloat16),
        in_specs=[anywhere] * 5,
        out_specs=anywhere,
        scratch_shapes=[
            pltpu.VMEM((2, rows, pulse_count), jnp.float32),
            *[pltpu.VMEM(array.shape, array.dtype) for array in operands],
            pltpu.VMEM((2 * INNER, outer), jnp.float32),
            pltpu.VMEM((rows, 2 * outer, INNER), jnp.bfloat16),
            pltpu.VMEM((rows, 2 * outer, INNER), jnp.bfloat16),
            pltpu.VMEM((rows * outer, 2 * INNER), jnp.bfloat16),
            pltpu.VMEM((rows * outer, 2 * INNER), jnp.bfloat16),
            pltpu.VMEM((2, rows, outer, INNER), jnp.bfloat16),
            pltpu.SemaphoreType.DMA((12,)),
        ],
        compiler_params=pltpu.CompilerParams(vmem_limit_bytes=VMEM_ALL),
        cost_estimate=pl.CostEstimate(flops=1000, bytes_accessed=1000, transcendentals=0),
        name="forward_dft",
    )(echoes, *operands)


def weights_kernel(shift, kernel, taps, weights):
    offsets, outer = weights.shape[0], weights.shape[1]
    half = INNER // 2
    tap_count = taps.shape[0]

    for parity in range(2):
        lanes = pl.ds(parity * half, half)
        shifts = shift[pl.ds(parity, half, stride=2), :].T
        kernels = kernel[pl.ds(parity, half, stride=2), :].T
        for start in range(0, outer, SUBLANES):
            here = slice(start, start + SUBLANES)
            moved = [
                jnp.take_along_axis(
                    jnp.broadcast_to(taps[pl.ds(tap, 1), :], (SUBLANES, LANES)),
                    kernels[here],
                    axis=1,
                )
                for tap in range(tap_count)
            ]
            moved += [jnp.zeros((SUBLANES, LANES), jnp.float32)] * (offsets - tap_count)
            for bit in reversed(range(SMAX.bit_length())):
                jump = 1 << bit
                taken = (shifts[here] & jump) != 0
                moved = [
                    jnp.where(taken, moved[row - jump] if row >= jump else 0.0, moved[row])
                    for row in range(offsets)
                ]
            for row in range(offsets):
                weights[row, pl.ds(start, SUBLANES), lanes] = moved[row]


def offset_weights(shift, kernel_index, taps):
    offsets = taps.shape[0] + SMAX
    inside = pl.BlockSpec(memory_space=pltpu.VMEM)
    return pl.pallas_call(
        weights_kernel,
        out_shape=jax.ShapeDtypeStruct((offsets, shift.shape[1], INNER), jnp.float32),
        in_specs=[inside] * 3,
        out_specs=inside,
        compiler_params=pltpu.CompilerParams(vmem_limit_bytes=VMEM_LIMIT),
        cost_estimate=pl.CostEstimate(flops=1000, bytes_accessed=1000, transcendentals=0),
        name="offset_weights",
    )(shift, kernel_index, taps)


def migrate(inputs, weights, lower, rows, store):
    offsets, outer = weights.shape[0], weights.shape[1]
    half = INNER // 2
    group = 2 * SUBLANES

    order = sorted(inputs, key=lambda number: number if lower else (number + 3) % 4)

    def body(step, carry):
        sub = pl.ds(pl.multiple_of(step * group, group), group)
        for parity in range(2):
            lanes = pl.ds(parity * half, half)
            for first in range(0, rows, ROW_GROUP):
                totals = [[None] * rows for _ in range(2)]
                held = {}
                for number in order:
                    for index in range(rows):
                        place = number * rows + index
                        wrap = 3 * rows if lower else 4 * rows * (number > 0)
                        pairs = [
                            (row, row - place + wrap) for row in range(first, first + ROW_GROUP)
                        ]
                        pairs = [pair for pair in pairs if 0 <= pair[1] < offsets]
                        if not pairs:
                            continue
                        values = [
                            inputs[number][part, index, sub, lanes].astype(jnp.float32)
                            for part in range(2)
                        ]
                        for row, offset in pairs:
                            if offset not in held:
                                held[offset] = weights[offset, sub, lanes]
                            for part in range(2):
                                term = held[offset] * values[part]
                                total = totals[part][row]
                                totals[part][row] = term if total is None else total + term
                for part in range(2):
                    for row in range(first, first + ROW_GROUP):
                        store(part, parity, row, sub, totals[part][row])
        return carry

    lax.fori_loop(0, outer // group, body, 0)


def by_half(odd_ref, lower_if_odd, run):
    odd = odd_ref[0] == 1

    @pl.when(odd)
    def _():
        run(lower_if_odd)

    @pl.when(jnp.logical_not(odd))
    def _():
        run(not lower_if_odd)


def partial_kernel(odd, *refs, numbers, lower_if_odd, has_partial):
    inputs = dict(zip(numbers, refs))
    earlier = refs[len(numbers)] if has_partial else None
    weights, out = refs[len(numbers) + has_partial :]
    half = INNER // 2

    def store(part, parity, row, place, total):
        lanes = pl.ds(parity * half, half)
        if has_partial:
            total = total + earlier[part, row, place, lanes]
        out[part, row, place, lanes] = total

    by_half(
        odd, lower_if_odd, lambda lower: migrate(inputs, weights, lower, out.shape[1], store)
    )


def partial(odd, blocks, lower_if_odd, weights, earlier):
    like = next(iter(blocks.values()))
    operands = [odd, *blocks.values(), *([] if earlier is None else [earlier]), weights]
    inside = pl.BlockSpec(memory_space=pltpu.VMEM)
    return pl.pallas_call(
        functools.partial(
            partial_kernel, numbers=tuple(blocks), lower_if_odd=lower_if_odd,
            has_partial=int(earlier is not None),
        ),
        out_shape=jax.ShapeDtypeStruct(like.shape, jnp.float32),
        in_specs=[pl.BlockSpec(memory_space=pltpu.SMEM)] + [inside] * (len(operands) - 1),
        out_specs=inside,
        compiler_params=pltpu.CompilerParams(vmem_limit_bytes=VMEM_LIMIT),
        cost_estimate=pl.CostEstimate(flops=1000, bytes_accessed=1000, transcendentals=0),
        name="migrate_known_rows",
    )(*operands)


def image_kernel(odd, *refs, numbers, lower_if_odd, has_partial, aliased):
    inputs = dict(zip(numbers, refs))
    count = len(numbers)
    earlier = refs[count] if has_partial else None
    weights, inner_table, outer_table, twiddle = refs[count + has_partial :][:4]
    out_hbm, migrated, images, out, semaphores = refs[count + has_partial + 4 + aliased :]
    rows = out.shape[1]
    pulse_count = out.shape[2]
    outer = pulse_count // INNER
    half = INNER // 2

    def store(part, parity, row, place, total):
        if has_partial:
            before = earlier[part, row, place, pl.ds(parity * half, half)]
            total = before if total is None else total + before
        migrated[row, place, pl.ds((2 * parity + part) * half, half)] = total.astype(jnp.bfloat16)

    by_half(odd, lower_if_odd, lambda lower: migrate(inputs, weights, lower, rows, store))
    cosine, sine = twiddle[0], twiddle[1]
    for start in range(0, rows, PER):
        left_parts, right_parts = (
            migrated[pl.ds(start, PER), :, pl.ds(parity * INNER, INNER)].reshape(PER * outer, INNER)
            for parity in range(2)
        )
        even = jnp.dot(left_parts, inner_table[0], preferred_element_type=jnp.float32)
        odd_bins = jnp.dot(right_parts, inner_table[1], preferred_element_type=jnp.float32)
        left, right = even + odd_bins, even - odd_bins
        for index in range(PER):
            here = slice(index * outer, (index + 1) * outer)
            turned = [], []
            for side, value in enumerate((left, right)):
                lanes = slice(side * half, (side + 1) * half)
                real, imag = value[here, :half], value[here, half:]
                turned[0].append(real * cosine[:, lanes] - imag * sine[:, lanes])
                turned[1].append(real * sine[:, lanes] + imag * cosine[:, lanes])
            turned = jnp.concatenate(
                [jnp.concatenate(pair, axis=1).astype(jnp.bfloat16) for pair in turned], axis=0
            )
            images[start + index] = jnp.dot(
                outer_table[...], turned, preferred_element_type=jnp.float32
            )
    chunks = 4
    chunk = pulse_count // chunks
    first_row = pl.multiple_of(jnp.where((odd[0] == 1) == lower_if_odd, 0, rows), rows)
    leaving = []
    for index in range(chunks):
        for part in range(2):
            for first_place in range(
                index * outer // chunks, (index + 1) * outer // chunks, SUBLANES
            ):
                swapped = jnp.swapaxes(
                    images[:, pl.ds(part * outer + first_place, SUBLANES), :], 0, 1
                )
                for offset in range(SUBLANES):
                    out[part, :, pl.ds((first_place + offset) * INNER, INNER)] = swapped[offset]
        place = pl.ds(index * chunk, chunk)
        leaving.append(
            pltpu.make_async_copy(
                out.at[:, :, place],
                out_hbm.at[:, pl.ds(first_row, rows), place],
                semaphores.at[index],
            )
        )
        leaving[-1].start()
    for copy in leaving:
        copy.wait()


def image(odd, blocks, lower_if_odd, weights, table, shape, earlier, previous):
    row_count, pulse_count = shape
    rows = SUBLANES
    outer = pulse_count // INNER
    operands = [
        odd, *blocks.values(), *([] if earlier is None else [earlier]), weights,
        table["inverse_inner"], table["inverse_outer"], table["twiddle"],
    ]
    specs = [pl.BlockSpec(memory_space=pltpu.SMEM)]
    specs += [pl.BlockSpec(memory_space=pltpu.VMEM)] * (len(operands) - 1)
    aliases = {}
    anywhere = pl.BlockSpec(memory_space=pl.ANY)
    if previous is not None:
        aliases = {len(operands): 0}
        operands.append(previous)
        specs.append(anywhere)
    return pl.pallas_call(
        functools.partial(
            image_kernel, numbers=tuple(blocks), lower_if_odd=lower_if_odd,
            has_partial=int(earlier is not None), aliased=len(aliases),
        ),
        out_shape=jax.ShapeDtypeStruct((2, row_count, pulse_count), jnp.float32),
        in_specs=specs,
        out_specs=anywhere,
        input_output_aliases=aliases,
        scratch_shapes=[
            pltpu.VMEM((rows, outer, 2 * INNER), jnp.bfloat16),
            pltpu.VMEM((rows, 2 * outer, INNER), jnp.float32),
            pltpu.VMEM((2, rows, pulse_count), jnp.float32),
            pltpu.SemaphoreType.DMA((4,)),
        ],
        compiler_params=pltpu.CompilerParams(vmem_limit_bytes=VMEM_LIMIT),
        cost_estimate=pl.CostEstimate(flops=1000, bytes_accessed=1000, transcendentals=0),
        name="migrate_and_image",
    )(*operands)


def per_device(echoes, doppler_filter, migration_shift, kernel_index, kernel_taps):
    row_count = echoes.shape[1]
    pulse_count = echoes.shape[2]
    outer = pulse_count // INNER
    table = tables(pulse_count)
    count = lax.axis_size("rng")
    odd = (lax.axis_index("rng") % 2).astype(jnp.int32).reshape(1)
    ahead = [(i, i + 1) for i in range(count - 1)]

    def swaps(first):
        pairs = [(i, i + 1) for i in range(first, count - 1, 2)]
        return pairs + [(j, i) for i, j in pairs]

    shape = (row_count, pulse_count)

    upper = forward(echoes, doppler_filter, table, 1)
    left_upper = lax.ppermute(upper, "rng", ahead)
    echoes, upper = lax.optimization_barrier((echoes, upper))
    lower = forward(echoes, doppler_filter, table, 0)
    near = lax.ppermute(lower, "rng", swaps(0))
    migration_shift, kernel_index, lower = lax.optimization_barrier(
        (migration_shift, kernel_index, lower)
    )
    shift = migration_shift.reshape(INNER, outer)
    index = kernel_index.reshape(INNER, outer)
    taps = jnp.pad(kernel_taps.T, ((0, 0), (0, LANES - kernel_taps.shape[0])))
    weights = offset_weights(shift, index, taps)
    rest = partial(odd, {2: lower}, False, weights, None)
    lower, rest = lax.optimization_barrier((lower, rest))
    far = lax.ppermute(lower, "rng", swaps(1))
    picture = image(
        odd, {0: near, 1: left_upper, 2: lower, 3: upper}, True, weights, table, shape, None, None
    )
    rest = partial(odd, {1: left_upper, 3: upper}, False, weights, rest)
    return image(odd, {0: far}, False, weights, table, shape, rest, picture)


def solution(mesh):
    return jax.shard_map(
        per_device,
        mesh=mesh,
        in_specs=(P(None, ("swath", "rng"), None), P(), P(), P(), P()),
        out_specs=P(None, ("swath", "rng"), None),
        check_vma=False,
    )
```

```python
import functools
import math

import jax
import jax.numpy as jnp
import numpy as np
from jax import lax
from jax.experimental import pallas as pl
from jax.experimental.pallas import tpu as pltpu
from jax.sharding import PartitionSpec as P

LANES = 128
INNER = 256
SUBLANES = 8
SMAX = 9
PER = 2
ROW_GROUP = 8
VMEM_LIMIT = 24 * 1024 * 1024
VMEM_ALL = 56 * 1024 * 1024


def split(values):
    high = values.astype(jnp.bfloat16)
    low = (values - high.astype(jnp.float32)).astype(jnp.bfloat16)
    return high, low


def dft_angles(length):
    numbers = np.arange(length, dtype=np.int64)
    return (numbers[:, None] * numbers[None, :] % length) * (2.0 * math.pi / length)


def np_split(values):
    values = values.astype(np.float32)
    high = values.astype(jnp.bfloat16)
    low = (values - high.astype(np.float32)).astype(jnp.bfloat16)
    return high, low


def tables(pulse_count):
    outer = pulse_count // INNER
    half = INNER // 2
    outer_angles = dft_angles(outer)
    oc, osn = np.cos(outer_angles), np.sin(outer_angles)
    places = np.arange(half, dtype=np.int64)
    forward_inner, inverse_inner = [], []
    for parity in range(2):
        angles = (places[:, None] * (2 * places[None, :] + parity) % INNER) * (
            2.0 * math.pi / INNER
        )
        ic, isn = np.cos(angles), np.sin(angles)
        forward_inner.append(np.stack(np_split(np.block([[ic, -isn], [isn, ic]]))))
        inverse_inner.append(np.block([[ic.T, isn.T], [-isn.T, ic.T]]).astype(jnp.bfloat16))
    forward_outer = np.block([[oc, osn], [-osn, oc]])
    inverse_outer = np.block([[oc, -osn], [osn, oc]])
    twist = (
        np.arange(outer, dtype=np.int64)[:, None] * np.arange(INNER, dtype=np.int64)[None, :]
    ) * (2.0 * math.pi / pulse_count)
    scale = 1.0 / math.sqrt(pulse_count)
    twiddle = np.stack([np.cos(twist), np.sin(twist)]) * scale
    return dict(
        forward_outer=np.stack(np_split(forward_outer)),
        forward_inner=np.stack(forward_inner),
        inverse_inner=np.stack(inverse_inner),
        inverse_outer=inverse_outer.astype(jnp.bfloat16),
        twiddle=twiddle.astype(np.float32),
    )


def forward_kernel(
    echo_hbm, outer_hbm, inner_hbm, twiddle_hbm, response_hbm, *refs, block
):
    (
        *targets, echo, outer_table, inner_table, twiddle, response, response_rows,
        signal_high, signal_low, rotated_high, rotated_low, out, semaphores,
    ) = refs
    rows = out.shape[1]
    pulse_count = echo.shape[2]
    outer = pulse_count // INNER
    half = INNER // 2
    chunks = 8
    chunk = pulse_count // chunks
    ready = [
        pltpu.make_async_copy(source, target, semaphores.at[index])
        for index, (source, target) in enumerate(
            [
                (response_hbm, response),
                (outer_hbm, outer_table),
                (twiddle_hbm, twiddle),
                (inner_hbm, inner_table),
            ]
        )
    ]
    for index in range(chunks):
        place = pl.ds(index * chunk, chunk)
        ready.append(
            pltpu.make_async_copy(
                echo_hbm.at[:, pl.ds(block * rows, rows), place],
                echo.at[:, :, place],
                semaphores.at[4 + index],
            )
        )
    for index in [0, *range(4, 4 + chunks), 1, 2, 3]:
        ready[index].start()
    ready[0].wait()
    for tile in range(INNER):
        response_rows[pl.ds(tile * 2, 2), :] = response[:, pl.ds(tile * outer, outer)]
    response_parts = [
        [response_rows[pl.ds(2 * parity + part, half, stride=4), :].T for part in range(2)]
        for parity in range(2)
    ]
    for index in range(chunks):
        ready[4 + index].wait()
        for part in range(2):
            for first in range(index * outer // chunks, (index + 1) * outer // chunks, SUBLANES):
                gathered = jnp.stack(
                    [
                        echo[part, :, pl.ds((first + offset) * INNER, INNER)]
                        for offset in range(SUBLANES)
                    ]
                )
                high, low = split(jnp.swapaxes(gathered, 0, 1))
                place = pl.ds(part * outer + first, SUBLANES)
                signal_high[:, place, :] = high
                signal_low[:, place, :] = low
    ready[1].wait()
    ready[2].wait()
    outer_high, outer_low = outer_table[0], outer_table[1]
    cosine, sine = twiddle[0], twiddle[1]

    def first_stage(row):
        high, low = signal_high[row], signal_low[row]
        sectioned = (
            jnp.dot(outer_high, low, preferred_element_type=jnp.float32)
            + jnp.dot(outer_low, high, preferred_element_type=jnp.float32)
            + jnp.dot(outer_high, high, preferred_element_type=jnp.float32)
        )
        real, imag = sectioned[:outer], sectioned[outer:]
        turned = (real * cosine + imag * sine, imag * cosine - real * sine)
        place = pl.ds(row * outer, outer)
        for part in range(2):
            left, right = turned[part][:, :half], turned[part][:, half:]
            for parity, value in enumerate((left + right, left - right)):
                high, low = split(value)
                lanes = pl.ds((2 * parity + part) * half, half)
                rotated_high[place, lanes] = high
                rotated_low[place, lanes] = low

    def second_stage(row):
        place = pl.ds(row * outer, PER * outer)
        for parity in range(2):
            lanes = pl.ds(parity * INNER, INNER)
            high = rotated_high[place, lanes]
            low = rotated_low[place, lanes]
            table_high, table_low = inner_table[parity, 0], inner_table[parity, 1]
            spectrum = (
                jnp.dot(high, table_low, preferred_element_type=jnp.float32)
                + jnp.dot(low, table_high, preferred_element_type=jnp.float32)
                + jnp.dot(high, table_high, preferred_element_type=jnp.float32)
            )
            response_real, response_imag = response_parts[parity]
            lanes = pl.ds(parity * half, half)
            for index in range(PER):
                real = spectrum[index * outer : (index + 1) * outer, :half]
                imag = spectrum[index * outer : (index + 1) * outer, half:]
                out[0, row + index, :, lanes] = (
                    real * response_real + imag * response_imag
                ).astype(jnp.bfloat16)
                out[1, row + index, :, lanes] = (
                    imag * response_real - real * response_imag
                ).astype(jnp.bfloat16)
        place = pl.ds(row, PER)
        length = targets[0].shape[1]
        leaving.append(
            pltpu.make_async_copy(
                out.at[:, place],
                targets[row // length].at[:, pl.ds(row % length, PER)],
                semaphores.at[4 + row // PER],
            )
        )
        leaving[-1].start()

    leaving = []
    for row in range(rows):
        first_stage(row)
        if row == 1:
            ready[3].wait()
        if row % PER == PER - 1 and row >= PER:
            second_stage(row + 1 - 2 * PER)
    second_stage(rows - PER)
    for copy in leaving:
        copy.wait()


def forward(echoes, doppler_filter, table, block, pieces):
    pulse_count = echoes.shape[2]
    rows = SUBLANES
    outer = pulse_count // INNER
    operands = [table["forward_outer"], table["forward_inner"], table["twiddle"], doppler_filter]
    anywhere = pl.BlockSpec(memory_space=pl.ANY)
    return pl.pallas_call(
        functools.partial(forward_kernel, block=block),
        out_shape=[
            jax.ShapeDtypeStruct((2, rows // pieces, outer, INNER), jnp.bfloat16)
            for _ in range(pieces)
        ],
        in_specs=[anywhere] * 5,
        out_specs=[anywhere] * pieces,
        scratch_shapes=[
            pltpu.VMEM((2, rows, pulse_count), jnp.float32),
            *[pltpu.VMEM(array.shape, array.dtype) for array in operands],
            pltpu.VMEM((2 * INNER, outer), jnp.float32),
            pltpu.VMEM((rows, 2 * outer, INNER), jnp.bfloat16),
            pltpu.VMEM((rows, 2 * outer, INNER), jnp.bfloat16),
            pltpu.VMEM((rows * outer, 2 * INNER), jnp.bfloat16),
            pltpu.VMEM((rows * outer, 2 * INNER), jnp.bfloat16),
            pltpu.VMEM((2, rows, outer, INNER), jnp.bfloat16),
            pltpu.SemaphoreType.DMA((12,)),
        ],
        compiler_params=pltpu.CompilerParams(vmem_limit_bytes=VMEM_ALL),
        cost_estimate=pl.CostEstimate(flops=10**12, bytes_accessed=10**9, transcendentals=0),
        name="forward_dft",
    )(echoes, *operands)


def weights_kernel(shift, kernel, taps, weights, ordered):
    offsets, outer = weights.shape[0], weights.shape[1]
    half = INNER // 2
    tap_count = taps.shape[0]

    for parity in range(2):
        lanes = pl.ds(parity * half, half)
        shifts = shift[pl.ds(parity, half, stride=2), :].T
        kernels = kernel[pl.ds(parity, half, stride=2), :].T
        ordered[:, lanes] = shifts.astype(jnp.float32).astype(jnp.bfloat16)
        for start in range(0, outer, SUBLANES):
            here = slice(start, start + SUBLANES)
            moved = [
                jnp.take_along_axis(
                    jnp.broadcast_to(taps[pl.ds(tap, 1), :], (SUBLANES, LANES)),
                    kernels[here],
                    axis=1,
                )
                for tap in range(tap_count)
            ]
            moved += [jnp.zeros((SUBLANES, LANES), jnp.float32)] * (offsets - tap_count)
            for bit in reversed(range(SMAX.bit_length())):
                jump = 1 << bit
                taken = (shifts[here] & jump) != 0
                moved = [
                    jnp.where(taken, moved[row - jump] if row >= jump else 0.0, moved[row])
                    for row in range(offsets)
                ]
            for row in range(offsets):
                weights[row, pl.ds(start, SUBLANES), lanes] = moved[row]


def offset_weights(shift, kernel_index, taps):
    offsets = taps.shape[0] + SMAX
    inside = pl.BlockSpec(memory_space=pltpu.VMEM)
    return pl.pallas_call(
        weights_kernel,
        out_shape=[
            jax.ShapeDtypeStruct((offsets, shift.shape[1], INNER), jnp.float32),
            jax.ShapeDtypeStruct((shift.shape[1], INNER), jnp.bfloat16),
        ],
        in_specs=[inside] * 3,
        out_specs=[inside] * 2,
        compiler_params=pltpu.CompilerParams(vmem_limit_bytes=VMEM_LIMIT),
        cost_estimate=pl.CostEstimate(flops=1000, bytes_accessed=1000, transcendentals=0),
        name="offset_weights",
    )(shift, kernel_index, taps)


def mix_kernel(odd, own, near, ordered, mixed):
    kept = mixed.shape[1]
    skipped = SUBLANES - kept

    def run(is_odd):
        left, right = (own, near) if is_odd else (near, own)
        for row in range(kept):
            for_next = ordered[...] >= jnp.bfloat16(SMAX - skipped - row)
            for part in range(2):
                mixed[part, row] = jnp.where(for_next, left[part, row], right[part, row])

    by_half(odd, True, run)


def mix(odd, own, near, ordered):
    inside = pl.BlockSpec(memory_space=pltpu.VMEM)
    return pl.pallas_call(
        mix_kernel,
        out_shape=jax.ShapeDtypeStruct(own.shape, own.dtype),
        in_specs=[pl.BlockSpec(memory_space=pltpu.SMEM)] + [inside] * 3,
        out_specs=inside,
        compiler_params=pltpu.CompilerParams(vmem_limit_bytes=VMEM_LIMIT),
        cost_estimate=pl.CostEstimate(flops=1000, bytes_accessed=1000, transcendentals=0),
        name="mix_rows",
    )(odd, own, near, ordered)


def migrate(inputs, weights, lower, rows, store):
    offsets, outer = weights.shape[0], weights.shape[1]
    half = INNER // 2
    group = 2 * SUBLANES

    order = sorted(inputs, key=lambda number: number if lower else (number + 3) % 4)

    def body(step, carry):
        sub = pl.ds(pl.multiple_of(step * group, group), group)
        for parity in range(2):
            lanes = pl.ds(parity * half, half)
            for first in range(0, rows, ROW_GROUP):
                totals = [[None] * rows for _ in range(2)]
                held = {}
                for number in order:
                    for index in range(rows):
                        place = number * rows + index
                        wrap = 3 * rows if lower else 4 * rows * (number > 0)
                        pairs = [
                            (row, row - place + wrap) for row in range(first, first + ROW_GROUP)
                        ]
                        pairs = [pair for pair in pairs if 0 <= pair[1] < offsets]
                        if not pairs:
                            continue
                        values = [
                            inputs[number](part, index, sub, lanes).astype(jnp.float32)
                            for part in range(2)
                        ]
                        for row, offset in pairs:
                            if offset not in held:
                                held[offset] = weights[offset, sub, lanes]
                            for part in range(2):
                                term = held[offset] * values[part]
                                total = totals[part][row]
                                totals[part][row] = term if total is None else total + term
                for part in range(2):
                    for row in range(first, first + ROW_GROUP):
                        store(part, parity, row, sub, totals[part][row])
        return carry

    lax.fori_loop(0, outer // group, body, 0)


def reader(pieces):
    length = pieces[0][0].shape[1]

    def read(part, index, sub, lanes):
        values = [ref[part, index % length, sub, lanes] for ref in pieces[index // length]]
        return sum(values[1:], values[0])

    return read


def readers(counts, refs):
    refs = iter(refs)
    return {
        number: reader([[next(refs) for _ in range(count)] for count in pieces])
        for number, pieces in counts
    }


def arrays_of(blocks):
    return [array for pieces in blocks.values() for piece in pieces for array in piece]


def counts_of(blocks):
    return tuple(
        (number, tuple(len(piece) for piece in pieces)) for number, pieces in blocks.items()
    )


def by_half(odd_ref, lower_if_odd, run):
    odd = odd_ref[0] == 1

    @pl.when(odd)
    def _():
        run(lower_if_odd)

    @pl.when(jnp.logical_not(odd))
    def _():
        run(not lower_if_odd)


def partial_kernel(odd, *refs, numbers, lower_if_odd, has_partial):
    inputs = readers(numbers, refs)
    count = sum(sum(pieces) for _, pieces in numbers)
    earlier = refs[count] if has_partial else None
    weights, out = refs[count + has_partial :]
    half = INNER // 2

    def store(part, parity, row, place, total):
        lanes = pl.ds(parity * half, half)
        if has_partial:
            total = total + earlier[part, row, place, lanes]
        out[part, row, place, lanes] = total

    by_half(
        odd, lower_if_odd, lambda lower: migrate(inputs, weights, lower, out.shape[1], store)
    )


def partial(odd, blocks, lower_if_odd, weights, earlier):
    shape = (2, SUBLANES) + weights.shape[1:]
    operands = [odd, *arrays_of(blocks), *([] if earlier is None else [earlier]), weights]
    inside = pl.BlockSpec(memory_space=pltpu.VMEM)
    return pl.pallas_call(
        functools.partial(
            partial_kernel, numbers=counts_of(blocks), lower_if_odd=lower_if_odd,
            has_partial=int(earlier is not None),
        ),
        out_shape=jax.ShapeDtypeStruct(shape, jnp.float32),
        in_specs=[pl.BlockSpec(memory_space=pltpu.SMEM)] + [inside] * (len(operands) - 1),
        out_specs=inside,
        compiler_params=pltpu.CompilerParams(vmem_limit_bytes=VMEM_LIMIT),
        cost_estimate=pl.CostEstimate(flops=1000, bytes_accessed=1000, transcendentals=0),
        name="migrate_known_rows",
    )(*operands)


def image_kernel(odd, *refs, numbers, lower_if_odd, has_partial, aliased):
    inputs = readers(numbers, refs)
    count = sum(sum(pieces) for _, pieces in numbers)
    earlier = refs[count] if has_partial else None
    weights, inner_table, outer_table, twiddle = refs[count + has_partial :][:4]
    out_hbm, migrated, images, out, semaphores = refs[count + has_partial + 4 + aliased :]
    rows = out.shape[1]
    pulse_count = out.shape[2]
    outer = pulse_count // INNER
    half = INNER // 2

    def store(part, parity, row, place, total):
        if has_partial:
            before = earlier[part, row, place, pl.ds(parity * half, half)]
            total = before if total is None else total + before
        migrated[row, place, pl.ds((2 * parity + part) * half, half)] = total.astype(jnp.bfloat16)

    by_half(odd, lower_if_odd, lambda lower: migrate(inputs, weights, lower, rows, store))
    cosine, sine = twiddle[0], twiddle[1]
    for start in range(0, rows, PER):
        left_parts, right_parts = (
            migrated[pl.ds(start, PER), :, pl.ds(parity * INNER, INNER)].reshape(PER * outer, INNER)
            for parity in range(2)
        )
        even = jnp.dot(left_parts, inner_table[0], preferred_element_type=jnp.float32)
        odd_bins = jnp.dot(right_parts, inner_table[1], preferred_element_type=jnp.float32)
        left, right = even + odd_bins, even - odd_bins
        for index in range(PER):
            here = slice(index * outer, (index + 1) * outer)
            turned = [], []
            for side, value in enumerate((left, right)):
                lanes = slice(side * half, (side + 1) * half)
                real, imag = value[here, :half], value[here, half:]
                turned[0].append(real * cosine[:, lanes] - imag * sine[:, lanes])
                turned[1].append(real * sine[:, lanes] + imag * cosine[:, lanes])
            turned = jnp.concatenate(
                [jnp.concatenate(pair, axis=1).astype(jnp.bfloat16) for pair in turned], axis=0
            )
            images[start + index] = jnp.dot(
                outer_table[...], turned, preferred_element_type=jnp.float32
            )
    chunks = 4
    chunk = pulse_count // chunks
    first_row = pl.multiple_of(jnp.where((odd[0] == 1) == lower_if_odd, 0, rows), rows)
    leaving = []
    for index in range(chunks):
        for part in range(2):
            for first_place in range(
                index * outer // chunks, (index + 1) * outer // chunks, SUBLANES
            ):
                swapped = jnp.swapaxes(
                    images[:, pl.ds(part * outer + first_place, SUBLANES), :], 0, 1
                )
                for offset in range(SUBLANES):
                    out[part, :, pl.ds((first_place + offset) * INNER, INNER)] = swapped[offset]
        place = pl.ds(index * chunk, chunk)
        leaving.append(
            pltpu.make_async_copy(
                out.at[:, :, place],
                out_hbm.at[:, pl.ds(first_row, rows), place],
                semaphores.at[index],
            )
        )
        leaving[-1].start()
    for copy in leaving:
        copy.wait()


def image(odd, blocks, lower_if_odd, weights, table, shape, earlier, previous):
    row_count, pulse_count = shape
    rows = SUBLANES
    outer = pulse_count // INNER
    operands = [
        odd, *arrays_of(blocks), *([] if earlier is None else [earlier]), weights,
        table["inverse_inner"], table["inverse_outer"], table["twiddle"],
    ]
    specs = [pl.BlockSpec(memory_space=pltpu.SMEM)]
    specs += [pl.BlockSpec(memory_space=pltpu.VMEM)] * (len(operands) - 1)
    aliases = {}
    anywhere = pl.BlockSpec(memory_space=pl.ANY)
    if previous is not None:
        aliases = {len(operands): 0}
        operands.append(previous)
        specs.append(anywhere)
    return pl.pallas_call(
        functools.partial(
            image_kernel, numbers=counts_of(blocks), lower_if_odd=lower_if_odd,
            has_partial=int(earlier is not None), aliased=len(aliases),
        ),
        out_shape=jax.ShapeDtypeStruct((2, row_count, pulse_count), jnp.float32),
        in_specs=specs,
        out_specs=anywhere,
        input_output_aliases=aliases,
        scratch_shapes=[
            pltpu.VMEM((rows, outer, 2 * INNER), jnp.bfloat16),
            pltpu.VMEM((rows, 2 * outer, INNER), jnp.float32),
            pltpu.VMEM((2, rows, pulse_count), jnp.float32),
            pltpu.SemaphoreType.DMA((4,)),
        ],
        compiler_params=pltpu.CompilerParams(vmem_limit_bytes=VMEM_LIMIT),
        cost_estimate=pl.CostEstimate(flops=1000, bytes_accessed=1000, transcendentals=0),
        name="migrate_and_image",
    )(*operands)


def per_device(echoes, doppler_filter, migration_shift, kernel_index, kernel_taps):
    row_count = echoes.shape[1]
    pulse_count = echoes.shape[2]
    outer = pulse_count // INNER
    table = tables(pulse_count)
    count = lax.axis_size("rng")
    odd = (lax.axis_index("rng") % 2).astype(jnp.int32).reshape(1)
    ahead = [(i, i + 1) for i in range(count - 1)]

    def swaps(first):
        pairs = [(i, i + 1) for i in range(first, count - 1, 2)]
        return pairs + [(j, i) for i, j in pairs]

    shape = (row_count, pulse_count)

    assert count % 4 == 0
    starts = range(0, count, 4)
    across = [(i + 1, i + 2) for i in starts] + [(i + 2, i + 1) for i in starts]
    onward = [(i + 2, i - 1) for i in starts[1:]] + [(i + 1, i + 4) for i in starts[:-1]]

    (upper,) = forward(echoes, doppler_filter, table, 1, 1)
    left_upper = lax.ppermute(upper, "rng", ahead)
    echoes, upper = lax.optimization_barrier((echoes, upper))
    few, many = forward(echoes, doppler_filter, table, 0, 2)
    near_many = lax.ppermute(many, "rng", swaps(0))
    near_few = lax.ppermute(few, "rng", swaps(0))
    migration_shift, kernel_index, few, many = lax.optimization_barrier(
        (migration_shift, kernel_index, few, many)
    )
    shift = migration_shift.reshape(INNER, outer)
    index = kernel_index.reshape(INNER, outer)
    taps = jnp.pad(kernel_taps.T, ((0, 0), (0, LANES - kernel_taps.shape[0])))
    weights, ordered = offset_weights(shift, index, taps)
    lower = ((few,), (many,))
    rest = partial(odd, {2: lower}, False, weights, None)
    mixed = mix(odd, many, near_many, ordered)
    mixed, rest = lax.optimization_barrier((mixed, rest))
    direct = lax.ppermute(mixed, "rng", across)
    rest = partial(odd, {1: ((left_upper,),), 3: ((upper,),)}, False, weights, rest)
    few, rest = lax.optimization_barrier((few, rest))
    far = lax.ppermute(few, "rng", swaps(1))
    relayed = lax.ppermute(direct, "rng", onward)
    few, direct = lax.optimization_barrier((few, direct))
    lower = ((few,), (many,))
    picture = image(
        odd,
        {0: ((near_few,), (near_many,)), 1: ((left_upper,),), 2: lower, 3: ((upper,),)},
        True, weights, table, shape, None, None,
    )
    return image(
        odd, {0: ((far,), (direct, relayed))}, False, weights, table, shape, rest, picture
    )


def solution(mesh):
    return jax.shard_map(
        per_device,
        mesh=mesh,
        in_specs=(P(None, ("swath", "rng"), None), P(), P(), P(), P()),
        out_specs=P(None, ("swath", "rng"), None),
        check_vma=False,
    )
```

```python
import functools
import math

import jax
import jax.numpy as jnp
import numpy as np
from jax import lax
from jax.experimental import pallas as pl
from jax.experimental.pallas import tpu as pltpu
from jax.sharding import PartitionSpec as P

LANES = 128
INNER = 256
SUBLANES = 8
SMAX = 9
PER = 2
ROW_GROUP = 8
VMEM_LIMIT = 24 * 1024 * 1024
VMEM_ALL = 56 * 1024 * 1024


def split(values):
    high = values.astype(jnp.bfloat16)
    low = (values - high.astype(jnp.float32)).astype(jnp.bfloat16)
    return high, low


def dft_angles(length):
    numbers = np.arange(length, dtype=np.int64)
    return (numbers[:, None] * numbers[None, :] % length) * (2.0 * math.pi / length)


def np_split(values):
    values = values.astype(np.float32)
    high = values.astype(jnp.bfloat16)
    low = (values - high.astype(np.float32)).astype(jnp.bfloat16)
    return high, low


def tables(pulse_count):
    outer = pulse_count // INNER
    half = INNER // 2
    outer_angles = dft_angles(outer)
    oc, osn = np.cos(outer_angles), np.sin(outer_angles)
    places = np.arange(half, dtype=np.int64)
    forward_inner, inverse_inner = [], []
    for parity in range(2):
        angles = (places[:, None] * (2 * places[None, :] + parity) % INNER) * (
            2.0 * math.pi / INNER
        )
        ic, isn = np.cos(angles), np.sin(angles)
        forward_inner.append(np.stack(np_split(np.block([[ic, -isn], [isn, ic]]))))
        inverse_inner.append(np.block([[ic.T, isn.T], [-isn.T, ic.T]]).astype(jnp.bfloat16))
    forward_outer = np.block([[oc, osn], [-osn, oc]])
    inverse_outer = np.block([[oc, -osn], [osn, oc]])
    twist = (
        np.arange(outer, dtype=np.int64)[:, None] * np.arange(INNER, dtype=np.int64)[None, :]
    ) * (2.0 * math.pi / pulse_count)
    scale = 1.0 / math.sqrt(pulse_count)
    twiddle = np.stack([np.cos(twist), np.sin(twist)]) * scale
    return dict(
        forward_outer=np.stack(np_split(forward_outer)),
        forward_inner=np.stack(forward_inner),
        inverse_inner=np.stack(inverse_inner),
        inverse_outer=inverse_outer.astype(jnp.bfloat16),
        twiddle=twiddle.astype(np.float32),
    )


def forward_kernel(
    echo_hbm, outer_hbm, inner_hbm, twiddle_hbm, response_hbm, *refs, block, copied
):
    (
        *targets, echo, outer_table, inner_table, twiddle, response, response_rows,
        signal_high, signal_low, rotated_high, rotated_low, semaphores,
    ) = refs[: len(refs) - copied]
    length = targets[0].shape[1]
    outs = [refs[-1]] if copied else targets
    rows = SUBLANES
    pulse_count = echo.shape[2]
    outer = pulse_count // INNER
    half = INNER // 2
    chunks = 8
    chunk = pulse_count // chunks
    ready = [
        pltpu.make_async_copy(source, target, semaphores.at[index])
        for index, (source, target) in enumerate(
            [
                (response_hbm, response),
                (outer_hbm, outer_table),
                (twiddle_hbm, twiddle),
                (inner_hbm, inner_table),
            ]
        )
    ]
    for index in range(chunks):
        place = pl.ds(index * chunk, chunk)
        ready.append(
            pltpu.make_async_copy(
                echo_hbm.at[:, pl.ds(block * rows, rows), place],
                echo.at[:, :, place],
                semaphores.at[4 + index],
            )
        )
    for index in [0, *range(4, 4 + chunks), 1, 2, 3]:
        ready[index].start()
    ready[0].wait()
    for tile in range(INNER):
        response_rows[pl.ds(tile * 2, 2), :] = response[:, pl.ds(tile * outer, outer)]
    response_parts = [
        [response_rows[pl.ds(2 * parity + part, half, stride=4), :].T for part in range(2)]
        for parity in range(2)
    ]
    for index in range(chunks):
        ready[4 + index].wait()
        for part in range(2):
            for first in range(index * outer // chunks, (index + 1) * outer // chunks, SUBLANES):
                gathered = jnp.stack(
                    [
                        echo[part, :, pl.ds((first + offset) * INNER, INNER)]
                        for offset in range(SUBLANES)
                    ]
                )
                high, low = split(jnp.swapaxes(gathered, 0, 1))
                place = pl.ds(part * outer + first, SUBLANES)
                signal_high[:, place, :] = high
                signal_low[:, place, :] = low
    ready[1].wait()
    ready[2].wait()
    outer_high, outer_low = outer_table[0], outer_table[1]
    cosine, sine = twiddle[0], twiddle[1]

    def first_stage(row):
        high, low = signal_high[row], signal_low[row]
        sectioned = (
            jnp.dot(outer_high, low, preferred_element_type=jnp.float32)
            + jnp.dot(outer_low, high, preferred_element_type=jnp.float32)
            + jnp.dot(outer_high, high, preferred_element_type=jnp.float32)
        )
        real, imag = sectioned[:outer], sectioned[outer:]
        turned = (real * cosine + imag * sine, imag * cosine - real * sine)
        place = pl.ds(row * outer, outer)
        for part in range(2):
            left, right = turned[part][:, :half], turned[part][:, half:]
            for parity, value in enumerate((left + right, left - right)):
                high, low = split(value)
                lanes = pl.ds((2 * parity + part) * half, half)
                rotated_high[place, lanes] = high
                rotated_low[place, lanes] = low

    def second_stage(row):
        place = pl.ds(row * outer, PER * outer)
        for parity in range(2):
            lanes = pl.ds(parity * INNER, INNER)
            high = rotated_high[place, lanes]
            low = rotated_low[place, lanes]
            table_high, table_low = inner_table[parity, 0], inner_table[parity, 1]
            spectrum = (
                jnp.dot(high, table_low, preferred_element_type=jnp.float32)
                + jnp.dot(low, table_high, preferred_element_type=jnp.float32)
                + jnp.dot(high, table_high, preferred_element_type=jnp.float32)
            )
            response_real, response_imag = response_parts[parity]
            lanes = pl.ds(parity * half, half)
            for index in range(PER):
                real = spectrum[index * outer : (index + 1) * outer, :half]
                imag = spectrum[index * outer : (index + 1) * outer, half:]
                out, slot = outs[(row + index) // length], (row + index) % length
                out[0, slot, :, lanes] = (
                    real * response_real + imag * response_imag
                ).astype(jnp.bfloat16)
                out[1, slot, :, lanes] = (
                    imag * response_real - real * response_imag
                ).astype(jnp.bfloat16)
        if copied:
            place = pl.ds(row, PER)
            leaving.append(
                pltpu.make_async_copy(
                    outs[0].at[:, place], targets[0].at[:, place], semaphores.at[4 + row // PER]
                )
            )
            leaving[-1].start()

    leaving = []
    for row in range(rows):
        first_stage(row)
        if row == 1:
            ready[3].wait()
        if row % PER == PER - 1 and row >= PER:
            second_stage(row + 1 - 2 * PER)
    second_stage(rows - PER)
    for copy in leaving:
        copy.wait()


def forward(echoes, doppler_filter, table, block, pieces, copied, limit):
    pulse_count = echoes.shape[2]
    rows = SUBLANES
    outer = pulse_count // INNER
    operands = [table["forward_outer"], table["forward_inner"], table["twiddle"], doppler_filter]
    anywhere = pl.BlockSpec(memory_space=pl.ANY)
    return pl.pallas_call(
        functools.partial(forward_kernel, block=block, copied=copied),
        out_shape=[
            jax.ShapeDtypeStruct((2, rows // pieces, outer, INNER), jnp.bfloat16)
            for _ in range(pieces)
        ],
        in_specs=[anywhere] * 5,
        out_specs=[anywhere if copied else pl.BlockSpec(memory_space=pltpu.VMEM)] * pieces,
        scratch_shapes=[
            pltpu.VMEM((2, rows, pulse_count), jnp.float32),
            *[pltpu.VMEM(array.shape, array.dtype) for array in operands],
            pltpu.VMEM((2 * INNER, outer), jnp.float32),
            pltpu.VMEM((rows, 2 * outer, INNER), jnp.bfloat16),
            pltpu.VMEM((rows, 2 * outer, INNER), jnp.bfloat16),
            pltpu.VMEM((rows * outer, 2 * INNER), jnp.bfloat16),
            pltpu.VMEM((rows * outer, 2 * INNER), jnp.bfloat16),
            pltpu.SemaphoreType.DMA((12,)),
        ]
        + [pltpu.VMEM((2, rows, outer, INNER), jnp.bfloat16)] * copied,
        compiler_params=pltpu.CompilerParams(vmem_limit_bytes=limit),
        cost_estimate=pl.CostEstimate(flops=10**12, bytes_accessed=10**9, transcendentals=0),
        name="forward_dft",
    )(echoes, *operands)


def weights_kernel(shift, kernel, taps, weights):
    offsets, outer = weights.shape[0], weights.shape[1]
    half = INNER // 2
    tap_count = taps.shape[0]

    for parity in range(2):
        lanes = pl.ds(parity * half, half)
        shifts = shift[pl.ds(parity, half, stride=2), :].T
        kernels = kernel[pl.ds(parity, half, stride=2), :].T
        for start in range(0, outer, SUBLANES):
            here = slice(start, start + SUBLANES)
            moved = [
                jnp.take_along_axis(
                    jnp.broadcast_to(taps[pl.ds(tap, 1), :], (SUBLANES, LANES)),
                    kernels[here],
                    axis=1,
                )
                for tap in range(tap_count)
            ]
            moved += [jnp.zeros((SUBLANES, LANES), jnp.float32)] * (offsets - tap_count)
            for bit in reversed(range(SMAX.bit_length())):
                jump = 1 << bit
                taken = (shifts[here] & jump) != 0
                moved = [
                    jnp.where(taken, moved[row - jump] if row >= jump else 0.0, moved[row])
                    for row in range(offsets)
                ]
            for row in range(offsets):
                weights[row, pl.ds(start, SUBLANES), lanes] = moved[row]


def offset_weights(shift, kernel_index, taps):
    offsets = taps.shape[0] + SMAX
    inside = pl.BlockSpec(memory_space=pltpu.VMEM)
    return pl.pallas_call(
        weights_kernel,
        out_shape=jax.ShapeDtypeStruct((offsets, shift.shape[1], INNER), jnp.float32),
        in_specs=[inside] * 3,
        out_specs=inside,
        compiler_params=pltpu.CompilerParams(vmem_limit_bytes=VMEM_LIMIT),
        cost_estimate=pl.CostEstimate(flops=1000, bytes_accessed=1000, transcendentals=0),
        name="offset_weights",
    )(shift, kernel_index, taps)


def mix_kernel(odd, own, near, shift, mixed):
    kept = mixed.shape[1]
    skipped = SUBLANES - kept
    half = INNER // 2

    def run(is_odd):
        left, right = (own, near) if is_odd else (near, own)
        for parity in range(2):
            lanes = pl.ds(parity * half, half)
            shifts = shift[pl.ds(parity, half, stride=2), :].T
            shifts = shifts.astype(jnp.float32).astype(jnp.bfloat16)
            for row in range(kept):
                for_next = shifts >= jnp.bfloat16(SMAX - skipped - row)
                for part in range(2):
                    mixed[part, row, :, lanes] = jnp.where(
                        for_next, left[part, row, :, lanes], right[part, row, :, lanes]
                    )

    by_half(odd, True, run)


def mix(odd, own, near, shift):
    inside = pl.BlockSpec(memory_space=pltpu.VMEM)
    return pl.pallas_call(
        mix_kernel,
        out_shape=jax.ShapeDtypeStruct(own.shape, own.dtype),
        in_specs=[pl.BlockSpec(memory_space=pltpu.SMEM)] + [inside] * 3,
        out_specs=inside,
        compiler_params=pltpu.CompilerParams(vmem_limit_bytes=VMEM_LIMIT),
        cost_estimate=pl.CostEstimate(flops=1000, bytes_accessed=1000, transcendentals=0),
        name="mix_rows",
    )(odd, own, near, shift)


def migrate(inputs, weights, lower, rows, store):
    offsets, outer = weights.shape[0], weights.shape[1]
    half = INNER // 2
    group = 2 * SUBLANES

    order = sorted(inputs, key=lambda number: number if lower else (number + 3) % 4)

    def body(step, carry):
        sub = pl.ds(pl.multiple_of(step * group, group), group)
        for parity in range(2):
            lanes = pl.ds(parity * half, half)
            for first in range(0, rows, ROW_GROUP):
                totals = [[None] * rows for _ in range(2)]
                held = {}
                for number in order:
                    for index in range(rows):
                        place = number * rows + index
                        wrap = 3 * rows if lower else 4 * rows * (number > 0)
                        pairs = [
                            (row, row - place + wrap) for row in range(first, first + ROW_GROUP)
                        ]
                        pairs = [pair for pair in pairs if 0 <= pair[1] < offsets]
                        if not pairs:
                            continue
                        values = [
                            inputs[number](part, index, sub, lanes).astype(jnp.float32)
                            for part in range(2)
                        ]
                        for row, offset in pairs:
                            if offset not in held:
                                held[offset] = weights[offset, sub, lanes]
                            for part in range(2):
                                term = held[offset] * values[part]
                                total = totals[part][row]
                                totals[part][row] = term if total is None else total + term
                for part in range(2):
                    for row in range(first, first + ROW_GROUP):
                        store(part, parity, row, sub, totals[part][row])
        return carry

    lax.fori_loop(0, outer // group, body, 0)


def reader(pieces):
    length = pieces[0][0].shape[1]

    def read(part, index, sub, lanes):
        values = [ref[part, index % length, sub, lanes] for ref in pieces[index // length]]
        return sum(values[1:], values[0])

    return read


def readers(counts, refs):
    refs = iter(refs)
    return {
        number: reader([[next(refs) for _ in range(count)] for count in pieces])
        for number, pieces in counts
    }


def arrays_of(blocks):
    return [array for pieces in blocks.values() for piece in pieces for array in piece]


def counts_of(blocks):
    return tuple(
        (number, tuple(len(piece) for piece in pieces)) for number, pieces in blocks.items()
    )


def by_half(odd_ref, lower_if_odd, run):
    odd = odd_ref[0] == 1

    @pl.when(odd)
    def _():
        run(lower_if_odd)

    @pl.when(jnp.logical_not(odd))
    def _():
        run(not lower_if_odd)


def partial_kernel(odd, *refs, numbers, lower_if_odd):
    inputs = readers(numbers, refs)
    weights, out = refs[-2:]
    half = INNER // 2

    def store(part, parity, row, place, total):
        lanes = pl.ds(parity * half, half)
        out[part, row, place, lanes] = total

    by_half(
        odd, lower_if_odd, lambda lower: migrate(inputs, weights, lower, out.shape[1], store)
    )


def partial(odd, blocks, lower_if_odd, weights):
    shape = (2, SUBLANES) + weights.shape[1:]
    operands = [odd, *arrays_of(blocks), weights]
    inside = pl.BlockSpec(memory_space=pltpu.VMEM)
    return pl.pallas_call(
        functools.partial(
            partial_kernel, numbers=counts_of(blocks), lower_if_odd=lower_if_odd
        ),
        out_shape=jax.ShapeDtypeStruct(shape, jnp.float32),
        in_specs=[pl.BlockSpec(memory_space=pltpu.SMEM)] + [inside] * (len(operands) - 1),
        out_specs=inside,
        compiler_params=pltpu.CompilerParams(vmem_limit_bytes=VMEM_LIMIT),
        cost_estimate=pl.CostEstimate(flops=1000, bytes_accessed=1000, transcendentals=0),
        name="migrate_known_rows",
    )(*operands)


def image_kernel(odd, *refs, numbers, lower_if_odd, other_numbers, aliased):
    inputs = readers(numbers, refs)
    count = sum(sum(pieces) for _, pieces in numbers)
    earlier, weights, inner_table, outer_table, twiddle = refs[count : count + 5]
    out_hbm, *rest, migrated, images, out, semaphores = refs[count + 5 + aliased :]
    rows = out.shape[1]
    pulse_count = out.shape[2]
    outer = pulse_count // INNER
    half = INNER // 2

    def store(part, parity, row, place, total):
        if not other_numbers:
            total = total + earlier[part, row, place, pl.ds(parity * half, half)]
        migrated[row, place, pl.ds((2 * parity + part) * half, half)] = total.astype(jnp.bfloat16)

    by_half(odd, lower_if_odd, lambda lower: migrate(inputs, weights, lower, rows, store))
    cosine, sine = twiddle[0], twiddle[1]
    for start in range(0, rows, PER):
        left_parts, right_parts = (
            migrated[pl.ds(start, PER), :, pl.ds(parity * INNER, INNER)].reshape(PER * outer, INNER)
            for parity in range(2)
        )
        even = jnp.dot(left_parts, inner_table[0], preferred_element_type=jnp.float32)
        odd_bins = jnp.dot(right_parts, inner_table[1], preferred_element_type=jnp.float32)
        left, right = even + odd_bins, even - odd_bins
        for index in range(PER):
            here = slice(index * outer, (index + 1) * outer)
            turned = [], []
            for side, value in enumerate((left, right)):
                lanes = slice(side * half, (side + 1) * half)
                real, imag = value[here, :half], value[here, half:]
                turned[0].append(real * cosine[:, lanes] - imag * sine[:, lanes])
                turned[1].append(real * sine[:, lanes] + imag * cosine[:, lanes])
            turned = jnp.concatenate(
                [jnp.concatenate(pair, axis=1).astype(jnp.bfloat16) for pair in turned], axis=0
            )
            images[start + index] = jnp.dot(
                outer_table[...], turned, preferred_element_type=jnp.float32
            )
    chunks = 4
    chunk = pulse_count // chunks
    first_row = pl.multiple_of(jnp.where((odd[0] == 1) == lower_if_odd, 0, rows), rows)
    leaving = []
    for index in range(chunks):
        for part in range(2):
            for first_place in range(
                index * outer // chunks, (index + 1) * outer // chunks, SUBLANES
            ):
                swapped = jnp.swapaxes(
                    images[:, pl.ds(part * outer + first_place, SUBLANES), :], 0, 1
                )
                for offset in range(SUBLANES):
                    out[part, :, pl.ds((first_place + offset) * INNER, INNER)] = swapped[offset]
        place = pl.ds(index * chunk, chunk)
        leaving.append(
            pltpu.make_async_copy(
                out.at[:, :, place],
                out_hbm.at[:, pl.ds(first_row, rows), place],
                semaphores.at[index],
            )
        )
        leaving[-1].start()
    if other_numbers:
        others = {number: inputs[number] for number in other_numbers}

        def store_rest(part, parity, row, place, total):
            lanes = pl.ds(parity * half, half)
            rest[0][part, row, place, lanes] = total + earlier[part, row, place, lanes]

        by_half(
            odd,
            not lower_if_odd,
            lambda lower: migrate(others, weights, lower, rows, store_rest),
        )
    for copy in leaving:
        copy.wait()


def image(odd, blocks, lower_if_odd, weights, table, shape, earlier, others, previous):
    row_count, pulse_count = shape
    rows = SUBLANES
    outer = pulse_count // INNER
    operands = [
        odd, *arrays_of(blocks), earlier, weights,
        table["inverse_inner"], table["inverse_outer"], table["twiddle"],
    ]
    specs = [pl.BlockSpec(memory_space=pltpu.SMEM)]
    specs += [pl.BlockSpec(memory_space=pltpu.VMEM)] * (len(operands) - 1)
    aliases = {}
    anywhere = pl.BlockSpec(memory_space=pl.ANY)
    if previous is not None:
        aliases = {len(operands): 0}
        operands.append(previous)
        specs.append(anywhere)
    return pl.pallas_call(
        functools.partial(
            image_kernel, numbers=counts_of(blocks), lower_if_odd=lower_if_odd,
            other_numbers=others, aliased=len(aliases),
        ),
        out_shape=[jax.ShapeDtypeStruct((2, row_count, pulse_count), jnp.float32)]
        + [jax.ShapeDtypeStruct(earlier.shape, earlier.dtype)] * bool(others),
        in_specs=specs,
        out_specs=[anywhere] + [pl.BlockSpec(memory_space=pltpu.VMEM)] * bool(others),
        input_output_aliases=aliases,
        scratch_shapes=[
            pltpu.VMEM((rows, outer, 2 * INNER), jnp.bfloat16),
            pltpu.VMEM((rows, 2 * outer, INNER), jnp.float32),
            pltpu.VMEM((2, rows, pulse_count), jnp.float32),
            pltpu.SemaphoreType.DMA((4,)),
        ],
        compiler_params=pltpu.CompilerParams(vmem_limit_bytes=VMEM_LIMIT),
        cost_estimate=pl.CostEstimate(flops=1000, bytes_accessed=1000, transcendentals=0),
        name="migrate_and_image",
    )(*operands)


def per_device(echoes, doppler_filter, migration_shift, kernel_index, kernel_taps):
    row_count = echoes.shape[1]
    pulse_count = echoes.shape[2]
    outer = pulse_count // INNER
    table = tables(pulse_count)
    count = lax.axis_size("rng")
    odd = (lax.axis_index("rng") % 2).astype(jnp.int32).reshape(1)
    ahead = [(i, i + 1) for i in range(count - 1)]

    def swaps(first):
        pairs = [(i, i + 1) for i in range(first, count - 1, 2)]
        return pairs + [(j, i) for i, j in pairs]

    shape = (row_count, pulse_count)

    assert count % 4 == 0
    starts = range(0, count, 4)
    across = [(i + 1, i + 2) for i in starts] + [(i + 2, i + 1) for i in starts]
    onward = [(i + 2, i - 1) for i in starts[1:]] + [(i + 1, i + 4) for i in starts[:-1]]

    (upper,) = forward(echoes, doppler_filter, table, 1, 1, True, VMEM_ALL)
    left_upper = lax.ppermute(upper, "rng", ahead)
    echoes, upper = lax.optimization_barrier((echoes, upper))
    few, many = forward(echoes, doppler_filter, table, 0, 2, False, VMEM_LIMIT)
    near_many = lax.ppermute(many, "rng", swaps(0))
    near_few = lax.ppermute(few, "rng", swaps(0))
    shift = migration_shift.reshape(INNER, outer)
    mixed = mix(odd, many, near_many, shift)
    direct = lax.ppermute(mixed, "rng", across)
    kernel_index, kernel_taps, mixed = lax.optimization_barrier(
        (kernel_index, kernel_taps, mixed)
    )
    index = kernel_index.reshape(INNER, outer)
    taps = jnp.pad(kernel_taps.T, ((0, 0), (0, LANES - kernel_taps.shape[0])))
    weights = offset_weights(shift, index, taps)
    rest = partial(odd, {2: ((few,), (many,))}, False, weights)
    few, rest, left_upper = lax.optimization_barrier((few, rest, left_upper))
    far = lax.ppermute(few, "rng", swaps(1))
    relayed = lax.ppermute(direct, "rng", onward)
    few, direct = lax.optimization_barrier((few, direct))
    picture, rest = image(
        odd,
        {
            0: ((near_few,), (near_many,)),
            1: ((left_upper,),),
            2: ((few,), (many,)),
            3: ((upper,),),
        },
        True, weights, table, shape, rest, (1, 3), None,
    )
    (picture,) = image(
        odd, {0: ((far,), (direct, relayed))}, False, weights, table, shape, rest, (), picture
    )
    return picture


def solution(mesh):
    return jax.shard_map(
        per_device,
        mesh=mesh,
        in_specs=(P(None, ("swath", "rng"), None), P(), P(), P(), P()),
        out_specs=P(None, ("swath", "rng"), None),
        check_vma=False,
    )
```

```python
import functools
import math

import jax
import jax.numpy as jnp
import numpy as np
from jax import lax
from jax.experimental import pallas as pl
from jax.experimental.pallas import tpu as pltpu
from jax.sharding import PartitionSpec as P

LANES = 128
INNER = 256
SUBLANES = 8
SMAX = 9
PER = 2
ROW_GROUP = 8
MERGED = 4
CHUNKS = 2
PIECES = 2
VMEM_LIMIT = 24 * 1024 * 1024
VMEM_ALL = 56 * 1024 * 1024


def split(values):
    high = values.astype(jnp.bfloat16)
    low = (values - high.astype(jnp.float32)).astype(jnp.bfloat16)
    return high, low


def dft_angles(length):
    numbers = np.arange(length, dtype=np.int64)
    return (numbers[:, None] * numbers[None, :] % length) * (2.0 * math.pi / length)


def np_split(values):
    values = values.astype(np.float32)
    high = values.astype(jnp.bfloat16)
    low = (values - high.astype(np.float32)).astype(jnp.bfloat16)
    return high, low


def tables(pulse_count):
    outer = pulse_count // INNER
    half = INNER // 2
    outer_angles = dft_angles(outer)
    oc, osn = np.cos(outer_angles), np.sin(outer_angles)
    places = np.arange(half, dtype=np.int64)
    forward_inner, inverse_inner = [], []
    for parity in range(2):
        angles = (places[:, None] * (2 * places[None, :] + parity) % INNER) * (
            2.0 * math.pi / INNER
        )
        ic, isn = np.cos(angles), np.sin(angles)
        forward_inner.append(np.stack(np_split(np.block([[ic, -isn], [isn, ic]]))))
        inverse_inner.append(np.block([[ic.T, isn.T], [-isn.T, ic.T]]).astype(jnp.bfloat16))
    forward_outer = np.block([[oc, osn], [-osn, oc]])
    length = outer // CHUNKS
    inverse_outer = np.concatenate(
        [
            np.block([[oc[here], -osn[here]], [osn[here], oc[here]]])
            for here in (slice(start, start + length) for start in range(0, outer, length))
        ]
    )
    twist = (
        np.arange(outer, dtype=np.int64)[:, None] * np.arange(INNER, dtype=np.int64)[None, :]
    ) * (2.0 * math.pi / pulse_count)
    scale = 1.0 / math.sqrt(pulse_count)
    twiddle = np.stack([np.cos(twist), np.sin(twist)]) * scale
    return dict(
        forward_outer=np.stack(np_split(forward_outer)),
        forward_inner=np.stack(forward_inner),
        inverse_inner=np.stack(inverse_inner),
        inverse_outer=inverse_outer.astype(jnp.bfloat16),
        twiddle=twiddle.astype(np.float32),
    )


def forward_kernel(
    echo_hbm, outer_hbm, inner_hbm, twiddle_hbm, response_hbm, *refs, block, copied
):
    (
        *targets, echo, outer_table, inner_table, twiddle, response, response_rows,
        signal_high, signal_low, rotated_high, rotated_low, semaphores,
    ) = refs[: len(refs) - copied]
    outs = [refs[-1]] if copied else targets
    slots = [(ref, slot) for ref in outs for slot in range(ref.shape[1])]
    rows = SUBLANES
    pulse_count = echo.shape[2]
    outer = pulse_count // INNER
    half = INNER // 2
    chunks = 8
    chunk = pulse_count // chunks
    ready = [
        pltpu.make_async_copy(source, target, semaphores.at[index])
        for index, (source, target) in enumerate(
            [
                (response_hbm, response),
                (outer_hbm, outer_table),
                (twiddle_hbm, twiddle),
                (inner_hbm, inner_table),
            ]
        )
    ]
    for index in range(chunks):
        place = pl.ds(index * chunk, chunk)
        ready.append(
            pltpu.make_async_copy(
                echo_hbm.at[:, pl.ds(block * rows, rows), place],
                echo.at[:, :, place],
                semaphores.at[4 + index],
            )
        )
    for index in [0, *range(4, 4 + chunks), 1, 2, 3]:
        ready[index].start()
    ready[0].wait()
    for tile in range(INNER):
        response_rows[pl.ds(tile * 2, 2), :] = response[:, pl.ds(tile * outer, outer)]
    response_parts = [
        [response_rows[pl.ds(2 * parity + part, half, stride=4), :].T for part in range(2)]
        for parity in range(2)
    ]
    for index in range(chunks):
        ready[4 + index].wait()
        for part in range(2):
            for first in range(index * outer // chunks, (index + 1) * outer // chunks, SUBLANES):
                gathered = jnp.stack(
                    [
                        echo[part, :, pl.ds((first + offset) * INNER, INNER)]
                        for offset in range(SUBLANES)
                    ]
                )
                high, low = split(jnp.swapaxes(gathered, 0, 1))
                place = pl.ds(part * outer + first, SUBLANES)
                signal_high[:, place, :] = high
                signal_low[:, place, :] = low
    ready[1].wait()
    ready[2].wait()
    outer_high, outer_low = outer_table[0], outer_table[1]
    cosine, sine = twiddle[0], twiddle[1]

    def first_stage(row):
        high, low = signal_high[row], signal_low[row]
        sectioned = (
            jnp.dot(outer_high, low, preferred_element_type=jnp.float32)
            + jnp.dot(outer_low, high, preferred_element_type=jnp.float32)
            + jnp.dot(outer_high, high, preferred_element_type=jnp.float32)
        )
        real, imag = sectioned[:outer], sectioned[outer:]
        turned = (real * cosine + imag * sine, imag * cosine - real * sine)
        place = pl.ds(row * outer, outer)
        for part in range(2):
            left, right = turned[part][:, :half], turned[part][:, half:]
            for parity, value in enumerate((left + right, left - right)):
                high, low = split(value)
                lanes = pl.ds((2 * parity + part) * half, half)
                rotated_high[place, lanes] = high
                rotated_low[place, lanes] = low

    def second_stage(row):
        place = pl.ds(row * outer, PER * outer)
        for parity in range(2):
            lanes = pl.ds(parity * INNER, INNER)
            high = rotated_high[place, lanes]
            low = rotated_low[place, lanes]
            table_high, table_low = inner_table[parity, 0], inner_table[parity, 1]
            spectrum = (
                jnp.dot(high, table_low, preferred_element_type=jnp.float32)
                + jnp.dot(low, table_high, preferred_element_type=jnp.float32)
                + jnp.dot(high, table_high, preferred_element_type=jnp.float32)
            )
            response_real, response_imag = response_parts[parity]
            lanes = pl.ds(parity * half, half)
            for index in range(PER):
                real = spectrum[index * outer : (index + 1) * outer, :half]
                imag = spectrum[index * outer : (index + 1) * outer, half:]
                out, slot = slots[row + index]
                out[0, slot, :, lanes] = (
                    real * response_real + imag * response_imag
                ).astype(jnp.bfloat16)
                out[1, slot, :, lanes] = (
                    imag * response_real - real * response_imag
                ).astype(jnp.bfloat16)
        if copied:
            place = pl.ds(row, PER)
            leaving.append(
                pltpu.make_async_copy(
                    outs[0].at[:, place], targets[0].at[:, place], semaphores.at[4 + row // PER]
                )
            )
            leaving[-1].start()

    leaving = []
    for row in range(rows):
        first_stage(row)
        if row == 1:
            ready[3].wait()
        if row % PER == PER - 1 and row >= PER:
            second_stage(row + 1 - 2 * PER)
    second_stage(rows - PER)
    for copy in leaving:
        copy.wait()


def forward(echoes, doppler_filter, table, block, lengths, copied, limit):
    pulse_count = echoes.shape[2]
    rows = SUBLANES
    outer = pulse_count // INNER
    operands = [table["forward_outer"], table["forward_inner"], table["twiddle"], doppler_filter]
    anywhere = pl.BlockSpec(memory_space=pl.ANY)
    return pl.pallas_call(
        functools.partial(forward_kernel, block=block, copied=copied),
        out_shape=[
            jax.ShapeDtypeStruct((2, length, outer, INNER), jnp.bfloat16) for length in lengths
        ],
        in_specs=[anywhere] * 5,
        out_specs=[anywhere if copied else pl.BlockSpec(memory_space=pltpu.VMEM)] * len(lengths),
        scratch_shapes=[
            pltpu.VMEM((2, rows, pulse_count), jnp.float32),
            *[pltpu.VMEM(array.shape, array.dtype) for array in operands],
            pltpu.VMEM((2 * INNER, outer), jnp.float32),
            pltpu.VMEM((rows, 2 * outer, INNER), jnp.bfloat16),
            pltpu.VMEM((rows, 2 * outer, INNER), jnp.bfloat16),
            pltpu.VMEM((rows * outer, 2 * INNER), jnp.bfloat16),
            pltpu.VMEM((rows * outer, 2 * INNER), jnp.bfloat16),
            pltpu.SemaphoreType.DMA((12,)),
        ]
        + [pltpu.VMEM((2, rows, outer, INNER), jnp.bfloat16)] * copied,
        compiler_params=pltpu.CompilerParams(vmem_limit_bytes=limit),
        cost_estimate=pl.CostEstimate(flops=10**12, bytes_accessed=10**9, transcendentals=0),
        name="forward_dft",
    )(echoes, *operands)


def weights_kernel(shift, kernel, taps, weights):
    offsets, outer = weights.shape[0], weights.shape[1]
    half = INNER // 2
    tap_count = taps.shape[0]

    for parity in range(2):
        lanes = pl.ds(parity * half, half)
        shifts = shift[pl.ds(parity, half, stride=2), :].T
        kernels = kernel[pl.ds(parity, half, stride=2), :].T
        for start in range(0, outer, SUBLANES):
            here = slice(start, start + SUBLANES)
            moved = [
                jnp.take_along_axis(
                    jnp.broadcast_to(taps[pl.ds(tap, 1), :], (SUBLANES, LANES)),
                    kernels[here],
                    axis=1,
                )
                for tap in range(tap_count)
            ]
            moved += [jnp.zeros((SUBLANES, LANES), jnp.float32)] * (offsets - tap_count)
            for bit in reversed(range(SMAX.bit_length())):
                jump = 1 << bit
                taken = (shifts[here] & jump) != 0
                moved = [
                    jnp.where(taken, moved[row - jump] if row >= jump else 0.0, moved[row])
                    for row in range(offsets)
                ]
            for row in range(offsets):
                weights[row, pl.ds(start, SUBLANES), lanes] = moved[row]


def offset_weights(shift, kernel_index, taps):
    offsets = taps.shape[0] + SMAX
    inside = pl.BlockSpec(memory_space=pltpu.VMEM)
    return pl.pallas_call(
        weights_kernel,
        out_shape=jax.ShapeDtypeStruct((offsets, shift.shape[1], INNER), jnp.float32),
        in_specs=[inside] * 3,
        out_specs=inside,
        compiler_params=pltpu.CompilerParams(vmem_limit_bytes=VMEM_LIMIT),
        cost_estimate=pl.CostEstimate(flops=1000, bytes_accessed=1000, transcendentals=0),
        name="offset_weights",
    )(shift, kernel_index, taps)


def mix_kernel(odd, own, near, shift, mixed):
    kept = mixed.shape[1]
    skipped = SUBLANES - kept
    half = INNER // 2

    def run(is_odd):
        left, right = (own, near) if is_odd else (near, own)
        for parity in range(2):
            lanes = pl.ds(parity * half, half)
            shifts = shift[pl.ds(parity, half, stride=2), :].T
            shifts = shifts.astype(jnp.float32).astype(jnp.bfloat16)
            for row in range(kept):
                for_next = shifts >= jnp.bfloat16(SMAX - skipped - row)
                for part in range(2):
                    mixed[part, row, :, lanes] = jnp.where(
                        for_next, left[part, row, :, lanes], right[part, row, :, lanes]
                    )

    by_half(odd, True, run)


def mix(odd, own, near, shift):
    inside = pl.BlockSpec(memory_space=pltpu.VMEM)
    return pl.pallas_call(
        mix_kernel,
        out_shape=jax.ShapeDtypeStruct(own.shape, own.dtype),
        in_specs=[pl.BlockSpec(memory_space=pltpu.SMEM)] + [inside] * 3,
        out_specs=inside,
        compiler_params=pltpu.CompilerParams(vmem_limit_bytes=VMEM_LIMIT),
        cost_estimate=pl.CostEstimate(flops=1000, bytes_accessed=1000, transcendentals=0),
        name="mix_rows",
    )(odd, own, near, shift)


def migrate(inputs, weights, lower, rows, store):
    offsets, outer = weights.shape[0], weights.shape[1]
    half = INNER // 2
    group = 2 * SUBLANES

    order = sorted(inputs, key=lambda number: number if lower else (number + 3) % 4)

    def body(step, carry):
        sub = pl.ds(pl.multiple_of(step * group, group), group)
        for parity in range(2):
            lanes = pl.ds(parity * half, half)
            for first in range(0, rows, ROW_GROUP):
                totals = [[None] * rows for _ in range(2)]
                held = {}
                for number in order:
                    for index in range(rows):
                        place = number * rows + index
                        wrap = 3 * rows if lower else 4 * rows * (number > 0)
                        pairs = [
                            (row, row - place + wrap) for row in range(first, first + ROW_GROUP)
                        ]
                        pairs = [pair for pair in pairs if 0 <= pair[1] < offsets]
                        if not pairs:
                            continue
                        values = [
                            inputs[number](part, index, sub, lanes).astype(jnp.float32)
                            for part in range(2)
                        ]
                        for row, offset in pairs:
                            if offset not in held:
                                held[offset] = weights[offset, sub, lanes]
                            for part in range(2):
                                term = held[offset] * values[part]
                                total = totals[part][row]
                                totals[part][row] = term if total is None else total + term
                for part in range(2):
                    for row in range(first, first + ROW_GROUP):
                        store(part, parity, row, sub, totals[part][row])
        return carry

    lax.fori_loop(0, outer // group, body, 0)


def reader(pieces):
    slots = [(piece, slot) for piece in pieces for slot in range(piece[0].shape[1])]

    def read(part, index, sub, lanes):
        piece, slot = slots[index]
        values = [ref[part, slot, sub, lanes] for ref in piece]
        return sum(values[1:], values[0])

    return read


def readers(counts, refs):
    refs = iter(refs)
    return {
        number: reader([[next(refs) for _ in range(count)] for count in pieces])
        for number, pieces in counts
    }


def arrays_of(blocks):
    return [array for pieces in blocks.values() for piece in pieces for array in piece]


def counts_of(blocks):
    return tuple(
        (number, tuple(len(piece) for piece in pieces)) for number, pieces in blocks.items()
    )


def by_half(odd_ref, lower_if_odd, run):
    odd = odd_ref[0] == 1

    @pl.when(odd)
    def _():
        run(lower_if_odd)

    @pl.when(jnp.logical_not(odd))
    def _():
        run(not lower_if_odd)


def partial_kernel(odd, *refs, numbers, lower_if_odd):
    inputs = readers(numbers, refs)
    weights, out = refs[-2:]
    half = INNER // 2

    def store(part, parity, row, place, total):
        lanes = pl.ds(parity * half, half)
        out[part, row, place, lanes] = total

    by_half(
        odd, lower_if_odd, lambda lower: migrate(inputs, weights, lower, out.shape[1], store)
    )


def partial(odd, blocks, lower_if_odd, weights):
    shape = (2, SUBLANES) + weights.shape[1:]
    operands = [odd, *arrays_of(blocks), weights]
    inside = pl.BlockSpec(memory_space=pltpu.VMEM)
    return pl.pallas_call(
        functools.partial(
            partial_kernel, numbers=counts_of(blocks), lower_if_odd=lower_if_odd
        ),
        out_shape=jax.ShapeDtypeStruct(shape, jnp.float32),
        in_specs=[pl.BlockSpec(memory_space=pltpu.SMEM)] + [inside] * (len(operands) - 1),
        out_specs=inside,
        compiler_params=pltpu.CompilerParams(vmem_limit_bytes=VMEM_LIMIT),
        cost_estimate=pl.CostEstimate(flops=1000, bytes_accessed=1000, transcendentals=0),
        name="migrate_known_rows",
    )(*operands)


def image_kernel(odd, *refs, numbers, lower_if_odd, other_numbers, aliased):
    inputs = readers(numbers, refs)
    count = sum(sum(pieces) for _, pieces in numbers)
    earlier, weights, inner_table, outer_table, twiddle = refs[count : count + 5]
    out_hbm, *rest, migrated, sections, images, out, semaphores = refs[count + 5 + aliased :]
    rows = out.shape[1]
    pulse_count = out.shape[2]
    outer = pulse_count // INNER
    half = INNER // 2

    def store(part, parity, row, place, total):
        if not other_numbers:
            total = total + earlier[part, row, place, pl.ds(parity * half, half)]
        migrated[row, place, pl.ds((2 * parity + part) * half, half)] = total.astype(jnp.bfloat16)

    by_half(odd, lower_if_odd, lambda lower: migrate(inputs, weights, lower, rows, store))
    cosine, sine = twiddle[0], twiddle[1]
    for start in range(0, rows, PER):
        left_parts, right_parts = (
            migrated[pl.ds(start, PER), :, pl.ds(parity * INNER, INNER)].reshape(PER * outer, INNER)
            for parity in range(2)
        )
        even = jnp.dot(left_parts, inner_table[0], preferred_element_type=jnp.float32)
        odd_bins = jnp.dot(right_parts, inner_table[1], preferred_element_type=jnp.float32)
        left, right = even + odd_bins, even - odd_bins
        for index in range(PER):
            here = slice(index * outer, (index + 1) * outer)
            turned = [], []
            for side, value in enumerate((left, right)):
                lanes = slice(side * half, (side + 1) * half)
                real, imag = value[here, :half], value[here, half:]
                turned[0].append(real * cosine[:, lanes] - imag * sine[:, lanes])
                turned[1].append(real * sine[:, lanes] + imag * cosine[:, lanes])
            for part in range(2):
                sections[start + index, pl.ds(part * outer, outer), :] = jnp.concatenate(
                    turned[part], axis=1
                ).astype(jnp.bfloat16)
    first_row = pl.multiple_of(jnp.where((odd[0] == 1) == lower_if_odd, 0, rows), rows)
    leaving = []
    length = outer // CHUNKS
    for chunk in range(CHUNKS):
        table = outer_table[pl.ds(2 * length * chunk, 2 * length), :]
        for row in range(rows):
            images[row, pl.ds(2 * length * chunk, 2 * length), :] = jnp.dot(
                table, sections[row], preferred_element_type=jnp.float32
            )
        for piece in range(PIECES):
            for part in range(2):
                for first_place in range(
                    piece * length // PIECES, (piece + 1) * length // PIECES, SUBLANES
                ):
                    swapped = jnp.swapaxes(
                        images[
                            :, pl.ds((2 * chunk + part) * length + first_place, SUBLANES), :
                        ],
                        0,
                        1,
                    )
                    for offset in range(SUBLANES):
                        lanes = pl.ds((chunk * length + first_place + offset) * INNER, INNER)
                        out[part, :, lanes] = swapped[offset]
            number = chunk * PIECES + piece
            place = pl.ds(number * (pulse_count // (CHUNKS * PIECES)), pulse_count // (CHUNKS * PIECES))
            leaving.append(
                pltpu.make_async_copy(
                    out.at[:, :, place],
                    out_hbm.at[:, pl.ds(first_row, rows), place],
                    semaphores.at[number],
                )
            )
            leaving[-1].start()
    if other_numbers:
        others = {number: inputs[number] for number in other_numbers}

        def store_rest(part, parity, row, place, total):
            lanes = pl.ds(parity * half, half)
            rest[0][part, row, place, lanes] = total + earlier[part, row, place, lanes]

        by_half(
            odd,
            not lower_if_odd,
            lambda lower: migrate(others, weights, lower, rows, store_rest),
        )
    for copy in leaving:
        copy.wait()


def image(odd, blocks, lower_if_odd, weights, table, shape, earlier, others, previous):
    row_count, pulse_count = shape
    rows = SUBLANES
    outer = pulse_count // INNER
    operands = [
        odd, *arrays_of(blocks), earlier, weights,
        table["inverse_inner"], table["inverse_outer"], table["twiddle"],
    ]
    specs = [pl.BlockSpec(memory_space=pltpu.SMEM)]
    specs += [pl.BlockSpec(memory_space=pltpu.VMEM)] * (len(operands) - 1)
    aliases = {}
    anywhere = pl.BlockSpec(memory_space=pl.ANY)
    if previous is not None:
        aliases = {len(operands): 0}
        operands.append(previous)
        specs.append(anywhere)
    return pl.pallas_call(
        functools.partial(
            image_kernel, numbers=counts_of(blocks), lower_if_odd=lower_if_odd,
            other_numbers=others, aliased=len(aliases),
        ),
        out_shape=[jax.ShapeDtypeStruct((2, row_count, pulse_count), jnp.float32)]
        + [jax.ShapeDtypeStruct(earlier.shape, earlier.dtype)] * bool(others),
        in_specs=specs,
        out_specs=[anywhere] + [pl.BlockSpec(memory_space=pltpu.VMEM)] * bool(others),
        input_output_aliases=aliases,
        scratch_shapes=[
            pltpu.VMEM((rows, outer, 2 * INNER), jnp.bfloat16),
            pltpu.VMEM((rows, 2 * outer, INNER), jnp.bfloat16),
            pltpu.VMEM((rows, 2 * outer, INNER), jnp.float32),
            pltpu.VMEM((2, rows, pulse_count), jnp.float32),
            pltpu.SemaphoreType.DMA((CHUNKS * PIECES,)),
        ],
        compiler_params=pltpu.CompilerParams(vmem_limit_bytes=VMEM_LIMIT),
        cost_estimate=pl.CostEstimate(flops=1000, bytes_accessed=1000, transcendentals=0),
        name="migrate_and_image",
    )(*operands)


def per_device(echoes, doppler_filter, migration_shift, kernel_index, kernel_taps):
    row_count = echoes.shape[1]
    pulse_count = echoes.shape[2]
    outer = pulse_count // INNER
    table = tables(pulse_count)
    count = lax.axis_size("rng")
    odd = (lax.axis_index("rng") % 2).astype(jnp.int32).reshape(1)
    ahead = [(i, i + 1) for i in range(count - 1)]

    def swaps(first):
        pairs = [(i, i + 1) for i in range(first, count - 1, 2)]
        return pairs + [(j, i) for i, j in pairs]

    shape = (row_count, pulse_count)

    assert count % 4 == 0
    starts = range(0, count, 4)
    across = [(i + 1, i + 2) for i in starts] + [(i + 2, i + 1) for i in starts]
    onward = [(i + 2, i - 1) for i in starts[1:]] + [(i + 1, i + 4) for i in starts[:-1]]

    (upper,) = forward(echoes, doppler_filter, table, 1, (SUBLANES,), True, VMEM_ALL)
    left_upper = lax.ppermute(upper, "rng", ahead)
    echoes, upper = lax.optimization_barrier((echoes, upper))
    lengths = (SUBLANES - MERGED, MERGED)
    few, many = forward(echoes, doppler_filter, table, 0, lengths, False, VMEM_LIMIT)
    near_many = lax.ppermute(many, "rng", swaps(0))
    near_few = lax.ppermute(few, "rng", swaps(0))
    shift = migration_shift.reshape(INNER, outer)
    mixed = mix(odd, many, near_many, shift)
    direct = lax.ppermute(mixed, "rng", across)
    kernel_index, kernel_taps, mixed = lax.optimization_barrier(
        (kernel_index, kernel_taps, mixed)
    )
    index = kernel_index.reshape(INNER, outer)
    taps = jnp.pad(kernel_taps.T, ((0, 0), (0, LANES - kernel_taps.shape[0])))
    weights = offset_weights(shift, index, taps)
    rest = partial(odd, {2: ((few,), (many,)), 3: ((upper,),)}, False, weights)
    few, rest, left_upper = lax.optimization_barrier((few, rest, left_upper))
    far = lax.ppermute(few, "rng", swaps(1))
    relayed = lax.ppermute(direct, "rng", onward)
    few, direct = lax.optimization_barrier((few, direct))
    picture, rest = image(
        odd,
        {
            0: ((near_few,), (near_many,)),
            1: ((left_upper,),),
            2: ((few,), (many,)),
            3: ((upper,),),
        },
        True, weights, table, shape, rest, (1,), None,
    )
    (picture,) = image(
        odd, {0: ((far,), (direct, relayed))}, False, weights, table, shape, rest, (), picture
    )
    return picture


def solution(mesh):
    return jax.shard_map(
        per_device,
        mesh=mesh,
        in_specs=(P(None, ("swath", "rng"), None), P(), P(), P(), P()),
        out_specs=P(None, ("swath", "rng"), None),
        check_vma=False,
    )
```

```python
import functools
import math

import jax
import jax.numpy as jnp
import numpy as np
from jax import lax
from jax.experimental import pallas as pl
from jax.experimental.pallas import tpu as pltpu
from jax.sharding import PartitionSpec as P

LANES = 128
INNER = 256
SUBLANES = 8
SMAX = 9
PER = 2
ROW_GROUP = 8
MERGED = 4
CHUNKS = 2
PIECES = 2
VMEM_LIMIT = 24 * 1024 * 1024
VMEM_ALL = 56 * 1024 * 1024


def split(values):
    high = values.astype(jnp.bfloat16)
    low = (values - high.astype(jnp.float32)).astype(jnp.bfloat16)
    return high, low


def dft_angles(length):
    numbers = np.arange(length, dtype=np.int64)
    return (numbers[:, None] * numbers[None, :] % length) * (2.0 * math.pi / length)


def np_split(values):
    values = values.astype(np.float32)
    high = values.astype(jnp.bfloat16)
    low = (values - high.astype(np.float32)).astype(jnp.bfloat16)
    return high, low


def tables(pulse_count):
    outer = pulse_count // INNER
    half = INNER // 2
    outer_angles = dft_angles(outer)
    oc, osn = np.cos(outer_angles), np.sin(outer_angles)
    places = np.arange(half, dtype=np.int64)
    forward_inner, inverse_inner = [], []
    for parity in range(2):
        angles = (places[:, None] * (2 * places[None, :] + parity) % INNER) * (
            2.0 * math.pi / INNER
        )
        ic, isn = np.cos(angles), np.sin(angles)
        forward_inner.append(np.stack(np_split(np.block([[ic, -isn], [isn, ic]]))))
        inverse_inner.append(np.block([[ic.T, isn.T], [-isn.T, ic.T]]).astype(jnp.bfloat16))
    forward_outer = np.block([[oc, osn], [-osn, oc]])
    length = outer // CHUNKS
    inverse_outer = np.concatenate(
        [
            np.block([[oc[here], -osn[here]], [osn[here], oc[here]]])
            for here in (slice(start, start + length) for start in range(0, outer, length))
        ]
    )
    twist = (
        np.arange(outer, dtype=np.int64)[:, None] * np.arange(INNER, dtype=np.int64)[None, :]
    ) * (2.0 * math.pi / pulse_count)
    scale = 1.0 / math.sqrt(pulse_count)
    twiddle = np.stack([np.cos(twist), np.sin(twist)]) * scale
    return dict(
        forward_outer=np.stack(np_split(forward_outer)),
        forward_inner=np.stack(forward_inner),
        inverse_inner=np.stack(inverse_inner),
        inverse_outer=inverse_outer.astype(jnp.bfloat16),
        twiddle=twiddle.astype(np.float32),
    )


def forward_kernel(
    echo_hbm, outer_hbm, inner_hbm, twiddle_hbm, response_hbm, *refs, block, copied
):
    (
        *targets, echo, outer_table, inner_table, twiddle, response, response_rows,
        signal_high, signal_low, rotated_high, rotated_low, semaphores,
    ) = refs[: len(refs) - copied]
    outs = [refs[-1]] if copied else targets
    slots = [(ref, slot) for ref in outs for slot in range(ref.shape[1])]
    rows = SUBLANES
    pulse_count = echo.shape[2]
    outer = pulse_count // INNER
    half = INNER // 2
    chunks = 8
    chunk = pulse_count // chunks
    ready = [
        pltpu.make_async_copy(source, target, semaphores.at[index])
        for index, (source, target) in enumerate(
            [
                (response_hbm, response),
                (outer_hbm, outer_table),
                (twiddle_hbm, twiddle),
                (inner_hbm, inner_table),
            ]
        )
    ]
    for index in range(chunks):
        place = pl.ds(index * chunk, chunk)
        ready.append(
            pltpu.make_async_copy(
                echo_hbm.at[:, pl.ds(block * rows, rows), place],
                echo.at[:, :, place],
                semaphores.at[4 + index],
            )
        )
    for index in [*range(4, 4 + chunks), 1, 2, 0, 3]:
        ready[index].start()
    for index in range(chunks):
        ready[4 + index].wait()
        for part in range(2):
            for first in range(index * outer // chunks, (index + 1) * outer // chunks, SUBLANES):
                gathered = jnp.stack(
                    [
                        echo[part, :, pl.ds((first + offset) * INNER, INNER)]
                        for offset in range(SUBLANES)
                    ]
                )
                high, low = split(jnp.swapaxes(gathered, 0, 1))
                place = pl.ds(part * outer + first, SUBLANES)
                signal_high[:, place, :] = high
                signal_low[:, place, :] = low
    ready[0].wait()
    for tile in range(INNER):
        response_rows[pl.ds(tile * 2, 2), :] = response[:, pl.ds(tile * outer, outer)]
    response_parts = [
        [response_rows[pl.ds(2 * parity + part, half, stride=4), :].T for part in range(2)]
        for parity in range(2)
    ]
    ready[1].wait()
    ready[2].wait()
    outer_high, outer_low = outer_table[0], outer_table[1]
    cosine, sine = twiddle[0], twiddle[1]

    def first_stage(row):
        high, low = signal_high[row], signal_low[row]
        sectioned = (
            jnp.dot(outer_high, low, preferred_element_type=jnp.float32)
            + jnp.dot(outer_low, high, preferred_element_type=jnp.float32)
            + jnp.dot(outer_high, high, preferred_element_type=jnp.float32)
        )
        real, imag = sectioned[:outer], sectioned[outer:]
        turned = (real * cosine + imag * sine, imag * cosine - real * sine)
        place = pl.ds(row * outer, outer)
        for part in range(2):
            left, right = turned[part][:, :half], turned[part][:, half:]
            for parity, value in enumerate((left + right, left - right)):
                high, low = split(value)
                lanes = pl.ds((2 * parity + part) * half, half)
                rotated_high[place, lanes] = high
                rotated_low[place, lanes] = low

    def second_stage(row):
        place = pl.ds(row * outer, PER * outer)
        for parity in range(2):
            lanes = pl.ds(parity * INNER, INNER)
            high = rotated_high[place, lanes]
            low = rotated_low[place, lanes]
            table_high, table_low = inner_table[parity, 0], inner_table[parity, 1]
            spectrum = (
                jnp.dot(high, table_low, preferred_element_type=jnp.float32)
                + jnp.dot(low, table_high, preferred_element_type=jnp.float32)
                + jnp.dot(high, table_high, preferred_element_type=jnp.float32)
            )
            response_real, response_imag = response_parts[parity]
            lanes = pl.ds(parity * half, half)
            for index in range(PER):
                real = spectrum[index * outer : (index + 1) * outer, :half]
                imag = spectrum[index * outer : (index + 1) * outer, half:]
                out, slot = slots[row + index]
                out[0, slot, :, lanes] = (
                    real * response_real + imag * response_imag
                ).astype(jnp.bfloat16)
                out[1, slot, :, lanes] = (
                    imag * response_real - real * response_imag
                ).astype(jnp.bfloat16)
        if copied:
            place = pl.ds(row, PER)
            leaving.append(
                pltpu.make_async_copy(
                    outs[0].at[:, place], targets[0].at[:, place], semaphores.at[4 + row // PER]
                )
            )
            leaving[-1].start()

    leaving = []
    for row in range(rows):
        first_stage(row)
        if row == 1:
            ready[3].wait()
        if row % PER == PER - 1 and row >= PER:
            second_stage(row + 1 - 2 * PER)
    second_stage(rows - PER)
    for copy in leaving:
        copy.wait()


def forward(echoes, doppler_filter, table, block, lengths, copied, limit):
    pulse_count = echoes.shape[2]
    rows = SUBLANES
    outer = pulse_count // INNER
    operands = [table["forward_outer"], table["forward_inner"], table["twiddle"], doppler_filter]
    anywhere = pl.BlockSpec(memory_space=pl.ANY)
    return pl.pallas_call(
        functools.partial(forward_kernel, block=block, copied=copied),
        out_shape=[
            jax.ShapeDtypeStruct((2, length, outer, INNER), jnp.bfloat16) for length in lengths
        ],
        in_specs=[anywhere] * 5,
        out_specs=[anywhere if copied else pl.BlockSpec(memory_space=pltpu.VMEM)] * len(lengths),
        scratch_shapes=[
            pltpu.VMEM((2, rows, pulse_count), jnp.float32),
            *[pltpu.VMEM(array.shape, array.dtype) for array in operands],
            pltpu.VMEM((2 * INNER, outer), jnp.float32),
            pltpu.VMEM((rows, 2 * outer, INNER), jnp.bfloat16),
            pltpu.VMEM((rows, 2 * outer, INNER), jnp.bfloat16),
            pltpu.VMEM((rows * outer, 2 * INNER), jnp.bfloat16),
            pltpu.VMEM((rows * outer, 2 * INNER), jnp.bfloat16),
            pltpu.SemaphoreType.DMA((12,)),
        ]
        + [pltpu.VMEM((2, rows, outer, INNER), jnp.bfloat16)] * copied,
        compiler_params=pltpu.CompilerParams(vmem_limit_bytes=limit),
        cost_estimate=pl.CostEstimate(flops=10**12, bytes_accessed=10**9, transcendentals=0),
        name="forward_dft",
    )(echoes, *operands)


def weights_kernel(shift, kernel, taps, weights):
    offsets, outer = weights.shape[0], weights.shape[1]
    half = INNER // 2
    tap_count = taps.shape[0]

    for parity in range(2):
        lanes = pl.ds(parity * half, half)
        shifts = shift[pl.ds(parity, half, stride=2), :].T
        kernels = kernel[pl.ds(parity, half, stride=2), :].T
        for start in range(0, outer, SUBLANES):
            here = slice(start, start + SUBLANES)
            moved = [
                jnp.take_along_axis(
                    jnp.broadcast_to(taps[pl.ds(tap, 1), :], (SUBLANES, LANES)),
                    kernels[here],
                    axis=1,
                )
                for tap in range(tap_count)
            ]
            moved += [jnp.zeros((SUBLANES, LANES), jnp.float32)] * (offsets - tap_count)
            for bit in reversed(range(SMAX.bit_length())):
                jump = 1 << bit
                taken = (shifts[here] & jump) != 0
                moved = [
                    jnp.where(taken, moved[row - jump] if row >= jump else 0.0, moved[row])
                    for row in range(offsets)
                ]
            for row in range(offsets):
                weights[row, pl.ds(start, SUBLANES), lanes] = moved[row]


def offset_weights(shift, kernel_index, taps):
    offsets = taps.shape[0] + SMAX
    inside = pl.BlockSpec(memory_space=pltpu.VMEM)
    return pl.pallas_call(
        weights_kernel,
        out_shape=jax.ShapeDtypeStruct((offsets, shift.shape[1], INNER), jnp.float32),
        in_specs=[inside] * 3,
        out_specs=inside,
        compiler_params=pltpu.CompilerParams(vmem_limit_bytes=VMEM_LIMIT),
        cost_estimate=pl.CostEstimate(flops=1000, bytes_accessed=1000, transcendentals=0),
        name="offset_weights",
    )(shift, kernel_index, taps)


def mix_kernel(odd, own, near, shift, mixed):
    kept = mixed.shape[1]
    skipped = SUBLANES - kept
    half = INNER // 2

    def run(is_odd):
        left, right = (own, near) if is_odd else (near, own)
        for parity in range(2):
            lanes = pl.ds(parity * half, half)
            shifts = shift[pl.ds(parity, half, stride=2), :].T
            shifts = shifts.astype(jnp.float32).astype(jnp.bfloat16)
            for row in range(kept):
                for_next = shifts >= jnp.bfloat16(SMAX - skipped - row)
                for part in range(2):
                    mixed[part, row, :, lanes] = jnp.where(
                        for_next, left[part, row, :, lanes], right[part, row, :, lanes]
                    )

    by_half(odd, True, run)


def mix(odd, own, near, shift):
    inside = pl.BlockSpec(memory_space=pltpu.VMEM)
    return pl.pallas_call(
        mix_kernel,
        out_shape=jax.ShapeDtypeStruct(own.shape, own.dtype),
        in_specs=[pl.BlockSpec(memory_space=pltpu.SMEM)] + [inside] * 3,
        out_specs=inside,
        compiler_params=pltpu.CompilerParams(vmem_limit_bytes=VMEM_LIMIT),
        cost_estimate=pl.CostEstimate(flops=1000, bytes_accessed=1000, transcendentals=0),
        name="mix_rows",
    )(odd, own, near, shift)


def migrate(inputs, weights, lower, rows, store):
    offsets, outer = weights.shape[0], weights.shape[1]
    half = INNER // 2
    group = 2 * SUBLANES

    order = sorted(inputs, key=lambda number: number if lower else (number + 3) % 4)

    def body(step, carry):
        sub = pl.ds(pl.multiple_of(step * group, group), group)
        for parity in range(2):
            lanes = pl.ds(parity * half, half)
            for first in range(0, rows, ROW_GROUP):
                totals = [[None] * rows for _ in range(2)]
                held = {}
                for number in order:
                    for index in range(rows):
                        place = number * rows + index
                        wrap = 3 * rows if lower else 4 * rows * (number > 0)
                        pairs = [
                            (row, row - place + wrap) for row in range(first, first + ROW_GROUP)
                        ]
                        pairs = [pair for pair in pairs if 0 <= pair[1] < offsets]
                        if not pairs:
                            continue
                        values = [
                            inputs[number](part, index, sub, lanes).astype(jnp.float32)
                            for part in range(2)
                        ]
                        for row, offset in pairs:
                            if offset not in held:
                                held[offset] = weights[offset, sub, lanes]
                            for part in range(2):
                                term = held[offset] * values[part]
                                total = totals[part][row]
                                totals[part][row] = term if total is None else total + term
                for part in range(2):
                    for row in range(first, first + ROW_GROUP):
                        store(part, parity, row, sub, totals[part][row])
        return carry

    lax.fori_loop(0, outer // group, body, 0)


def reader(pieces):
    slots = [(piece, slot) for piece in pieces for slot in range(piece[0].shape[1])]

    def read(part, index, sub, lanes):
        piece, slot = slots[index]
        values = [ref[part, slot, sub, lanes] for ref in piece]
        return sum(values[1:], values[0])

    return read


def readers(counts, refs):
    refs = iter(refs)
    return {
        number: reader([[next(refs) for _ in range(count)] for count in pieces])
        for number, pieces in counts
    }


def arrays_of(blocks):
    return [array for pieces in blocks.values() for piece in pieces for array in piece]


def counts_of(blocks):
    return tuple(
        (number, tuple(len(piece) for piece in pieces)) for number, pieces in blocks.items()
    )


def by_half(odd_ref, lower_if_odd, run):
    odd = odd_ref[0] == 1

    @pl.when(odd)
    def _():
        run(lower_if_odd)

    @pl.when(jnp.logical_not(odd))
    def _():
        run(not lower_if_odd)


def partial_kernel(odd, *refs, numbers, lower_if_odd):
    inputs = readers(numbers, refs)
    weights, out = refs[-2:]
    half = INNER // 2

    def store(part, parity, row, place, total):
        lanes = pl.ds(parity * half, half)
        out[part, row, place, lanes] = total

    by_half(
        odd, lower_if_odd, lambda lower: migrate(inputs, weights, lower, out.shape[1], store)
    )


def partial(odd, blocks, lower_if_odd, weights):
    shape = (2, SUBLANES) + weights.shape[1:]
    operands = [odd, *arrays_of(blocks), weights]
    inside = pl.BlockSpec(memory_space=pltpu.VMEM)
    return pl.pallas_call(
        functools.partial(
            partial_kernel, numbers=counts_of(blocks), lower_if_odd=lower_if_odd
        ),
        out_shape=jax.ShapeDtypeStruct(shape, jnp.float32),
        in_specs=[pl.BlockSpec(memory_space=pltpu.SMEM)] + [inside] * (len(operands) - 1),
        out_specs=inside,
        compiler_params=pltpu.CompilerParams(vmem_limit_bytes=VMEM_LIMIT),
        cost_estimate=pl.CostEstimate(flops=1000, bytes_accessed=1000, transcendentals=0),
        name="migrate_known_rows",
    )(*operands)


def image_kernel(odd, *refs, numbers, lower_if_odd, other_numbers, aliased):
    inputs = readers(numbers, refs)
    count = sum(sum(pieces) for _, pieces in numbers)
    earlier, weights, inner_table, outer_table, twiddle = refs[count : count + 5]
    out_hbm, *rest, migrated, sections, images, out, semaphores = refs[count + 5 + aliased :]
    rows = out.shape[1]
    pulse_count = out.shape[2]
    outer = pulse_count // INNER
    half = INNER // 2

    def store(part, parity, row, place, total):
        if not other_numbers:
            total = total + earlier[part, row, place, pl.ds(parity * half, half)]
        migrated[row, place, pl.ds((2 * parity + part) * half, half)] = total.astype(jnp.bfloat16)

    by_half(odd, lower_if_odd, lambda lower: migrate(inputs, weights, lower, rows, store))
    cosine, sine = twiddle[0], twiddle[1]
    for start in range(0, rows, PER):
        left_parts, right_parts = (
            migrated[pl.ds(start, PER), :, pl.ds(parity * INNER, INNER)].reshape(PER * outer, INNER)
            for parity in range(2)
        )
        even = jnp.dot(left_parts, inner_table[0], preferred_element_type=jnp.float32)
        odd_bins = jnp.dot(right_parts, inner_table[1], preferred_element_type=jnp.float32)
        left, right = even + odd_bins, even - odd_bins
        for index in range(PER):
            here = slice(index * outer, (index + 1) * outer)
            turned = [], []
            for side, value in enumerate((left, right)):
                lanes = slice(side * half, (side + 1) * half)
                real, imag = value[here, :half], value[here, half:]
                turned[0].append(real * cosine[:, lanes] - imag * sine[:, lanes])
                turned[1].append(real * sine[:, lanes] + imag * cosine[:, lanes])
            for part in range(2):
                sections[start + index, pl.ds(part * outer, outer), :] = jnp.concatenate(
                    turned[part], axis=1
                ).astype(jnp.bfloat16)
    first_row = pl.multiple_of(jnp.where((odd[0] == 1) == lower_if_odd, 0, rows), rows)
    leaving = []
    length = outer // CHUNKS
    for chunk in range(CHUNKS):
        table = outer_table[pl.ds(2 * length * chunk, 2 * length), :]
        for row in range(rows):
            images[row, pl.ds(2 * length * chunk, 2 * length), :] = jnp.dot(
                table, sections[row], preferred_element_type=jnp.float32
            )
        for piece in range(PIECES):
            for part in range(2):
                for first_place in range(
                    piece * length // PIECES, (piece + 1) * length // PIECES, SUBLANES
                ):
                    swapped = jnp.swapaxes(
                        images[
                            :, pl.ds((2 * chunk + part) * length + first_place, SUBLANES), :
                        ],
                        0,
                        1,
                    )
                    for offset in range(SUBLANES):
                        lanes = pl.ds((chunk * length + first_place + offset) * INNER, INNER)
                        out[part, :, lanes] = swapped[offset]
            number = chunk * PIECES + piece
            place = pl.ds(number * (pulse_count // (CHUNKS * PIECES)), pulse_count // (CHUNKS * PIECES))
            leaving.append(
                pltpu.make_async_copy(
                    out.at[:, :, place],
                    out_hbm.at[:, pl.ds(first_row, rows), place],
                    semaphores.at[number],
                )
            )
            leaving[-1].start()
    if other_numbers:
        others = {number: inputs[number] for number in other_numbers}

        def store_rest(part, parity, row, place, total):
            lanes = pl.ds(parity * half, half)
            rest[0][part, row, place, lanes] = total + earlier[part, row, place, lanes]

        by_half(
            odd,
            not lower_if_odd,
            lambda lower: migrate(others, weights, lower, rows, store_rest),
        )
    for copy in leaving:
        copy.wait()


def image(odd, blocks, lower_if_odd, weights, table, shape, earlier, others, previous):
    row_count, pulse_count = shape
    rows = SUBLANES
    outer = pulse_count // INNER
    operands = [
        odd, *arrays_of(blocks), earlier, weights,
        table["inverse_inner"], table["inverse_outer"], table["twiddle"],
    ]
    specs = [pl.BlockSpec(memory_space=pltpu.SMEM)]
    specs += [pl.BlockSpec(memory_space=pltpu.VMEM)] * (len(operands) - 1)
    aliases = {}
    anywhere = pl.BlockSpec(memory_space=pl.ANY)
    if previous is not None:
        aliases = {len(operands): 0}
        operands.append(previous)
        specs.append(anywhere)
    return pl.pallas_call(
        functools.partial(
            image_kernel, numbers=counts_of(blocks), lower_if_odd=lower_if_odd,
            other_numbers=others, aliased=len(aliases),
        ),
        out_shape=[jax.ShapeDtypeStruct((2, row_count, pulse_count), jnp.float32)]
        + [jax.ShapeDtypeStruct(earlier.shape, earlier.dtype)] * bool(others),
        in_specs=specs,
        out_specs=[anywhere] + [pl.BlockSpec(memory_space=pltpu.VMEM)] * bool(others),
        input_output_aliases=aliases,
        scratch_shapes=[
            pltpu.VMEM((rows, outer, 2 * INNER), jnp.bfloat16),
            pltpu.VMEM((rows, 2 * outer, INNER), jnp.bfloat16),
            pltpu.VMEM((rows, 2 * outer, INNER), jnp.float32),
            pltpu.VMEM((2, rows, pulse_count), jnp.float32),
            pltpu.SemaphoreType.DMA((CHUNKS * PIECES,)),
        ],
        compiler_params=pltpu.CompilerParams(vmem_limit_bytes=VMEM_LIMIT),
        cost_estimate=pl.CostEstimate(flops=1000, bytes_accessed=1000, transcendentals=0),
        name="migrate_and_image",
    )(*operands)


def per_device(echoes, doppler_filter, migration_shift, kernel_index, kernel_taps):
    row_count = echoes.shape[1]
    pulse_count = echoes.shape[2]
    outer = pulse_count // INNER
    table = tables(pulse_count)
    count = lax.axis_size("rng")
    odd = (lax.axis_index("rng") % 2).astype(jnp.int32).reshape(1)
    ahead = [(i, i + 1) for i in range(count - 1)]

    def swaps(first):
        pairs = [(i, i + 1) for i in range(first, count - 1, 2)]
        return pairs + [(j, i) for i, j in pairs]

    shape = (row_count, pulse_count)

    assert count % 4 == 0
    starts = range(0, count, 4)
    across = [(i + 1, i + 2) for i in starts] + [(i + 2, i + 1) for i in starts]
    onward = [(i + 2, i - 1) for i in starts[1:]] + [(i + 1, i + 4) for i in starts[:-1]]

    (upper,) = forward(echoes, doppler_filter, table, 1, (SUBLANES,), True, VMEM_ALL)
    left_upper = lax.ppermute(upper, "rng", ahead)
    echoes, upper = lax.optimization_barrier((echoes, upper))
    lengths = (SUBLANES - MERGED, MERGED)
    few, many = forward(echoes, doppler_filter, table, 0, lengths, False, VMEM_LIMIT)
    near_many = lax.ppermute(many, "rng", swaps(0))
    near_few = lax.ppermute(few, "rng", swaps(0))
    shift = migration_shift.reshape(INNER, outer)
    mixed = mix(odd, many, near_many, shift)
    direct = lax.ppermute(mixed, "rng", across)
    kernel_index, kernel_taps, mixed = lax.optimization_barrier(
        (kernel_index, kernel_taps, mixed)
    )
    index = kernel_index.reshape(INNER, outer)
    taps = jnp.pad(kernel_taps.T, ((0, 0), (0, LANES - kernel_taps.shape[0])))
    weights = offset_weights(shift, index, taps)
    rest = partial(odd, {2: ((few,), (many,)), 3: ((upper,),)}, False, weights)
    few, rest, left_upper = lax.optimization_barrier((few, rest, left_upper))
    far = lax.ppermute(few, "rng", swaps(1))
    relayed = lax.ppermute(direct, "rng", onward)
    few, direct = lax.optimization_barrier((few, direct))
    picture, rest = image(
        odd,
        {
            0: ((near_few,), (near_many,)),
            1: ((left_upper,),),
            2: ((few,), (many,)),
            3: ((upper,),),
        },
        True, weights, table, shape, rest, (1,), None,
    )
    (picture,) = image(
        odd, {0: ((far,), (direct, relayed))}, False, weights, table, shape, rest, (), picture
    )
    return picture


def solution(mesh):
    return jax.shard_map(
        per_device,
        mesh=mesh,
        in_specs=(P(None, ("swath", "rng"), None), P(), P(), P(), P()),
        out_specs=P(None, ("swath", "rng"), None),
        check_vma=False,
    )
```
